32 devices in a mesh: blk: 2 (over core), team: 16 (over z, y, x).
Axes of the slice: x: 2, y: 2, z: 4, core: 2. Of those that a mesh axis runs over, the one named last changes fastest.
Arguments:
- features: bfloat16 [4096, 256], P(('blk', 'team')), may hold values from -6 to 6
- weight: bfloat16 [256, 256], replicated, may hold values from -0.375 to 0.375
- bias: float32 [256], replicated, may hold values from -3 to 3
- cotangent: bfloat16 [4096, 256], P(('blk', 'team')), may hold values from -6 to 6
- adj_cols: int32 [16, 2, 2, 12], P('team', None, 'blk'), may hold values from 0 to 15, as said below
- adj_vals: bfloat16 [16, 2, 2, 12, 128, 128], P('team', None, 'blk'), as said below
Outputs:
- hidden: bfloat16 [4096, 256], P(('blk', 'team'))
- grad_input: bfloat16 [4096, 256], P(('blk', 'team'))
- grad_weight: float32 [256, 256], replicated
- grad_bias: float32 [256], replicated
The draws below stay inside these ranges and needn't reach their ends.
Inputs may be any that keep to these rules, and one draw needn't show every extreme that they name: `adj_cols`: for every node panel and column group the 12 entries are distinct. Block (i, j) of A is listed exactly when block (j, i) is, every column panel is listed by exactly 12 row panels of each column group, and A is symmetric. `adj_vals`: the block listed for panels (i, j) is the transpose of the block listed for (j, i), so A is symmetric.
All inputs are finite; a program needn't handle non-finite values.
Results may differ from the reference program's by a relative error of at most 0.0075.
Values may be sent and summed in bfloat16 or wider, within the bound.
A program may use at most 64 MiB of HBM per device.

```python
import jax
import jax.numpy as jnp
from jax import lax

BLOCK = 128
WIDTH = 256
NNZ = 12
GROUPS = 2
MEMBERS = 16
NODES = 4096


def pattern_parts(key):
    perm_keys = jax.random.split(jax.random.fold_in(key, 101), GROUPS)
    perms = jax.vmap(lambda one: jax.random.permutation(one, MEMBERS))(perm_keys).astype(jnp.int32)
    inverse = jnp.argsort(perms, axis=1).astype(jnp.int32)
    row_groups = jnp.arange(GROUPS, dtype=jnp.int32)[:, None]
    col_groups = jnp.arange(GROUPS, dtype=jnp.int32)[None, :]
    pair_ids = (jnp.minimum(row_groups, col_groups) * GROUPS + jnp.maximum(row_groups, col_groups)).reshape(-1)
    offset_key = jax.random.fold_in(key, 102)
    offsets = jax.vmap(lambda pair: jax.random.permutation(jax.random.fold_in(offset_key, pair), MEMBERS)[:NNZ])(pair_ids)
    offsets = offsets.reshape(GROUPS, GROUPS, NNZ).astype(jnp.int32)
    shifted = (offsets[None, :, :, :] - perms.T[:, :, None, None]) % MEMBERS
    group_ids = jnp.arange(GROUPS, dtype=jnp.int32)[None, None, :, None]
    return inverse[group_ids, shifted].astype(jnp.int32)


def draw_adj_cols(key, part):
    return pattern_parts(key)


def draw_adj_vals(key, part):
    columns = pattern_parts(key)
    value_key = jax.random.fold_in(key, 103)
    total_panels = GROUPS * MEMBERS
    row_panel = jnp.arange(GROUPS, dtype=jnp.int32)[None, :, None, None] * MEMBERS + jnp.arange(MEMBERS, dtype=jnp.int32)[:, None, None, None]
    col_panel = jnp.arange(GROUPS, dtype=jnp.int32)[None, None, :, None] * MEMBERS + columns
    row_panel = jnp.broadcast_to(row_panel, columns.shape)
    lower = jnp.minimum(row_panel, col_panel)
    upper = jnp.maximum(row_panel, col_panel)
    flipped = row_panel > col_panel
    same = row_panel == col_panel
    factor = (BLOCK * NNZ * GROUPS) ** (-0.5)

    def one_block(entry):
        low_id, high_id, flip, diag = entry
        block_key = jax.random.fold_in(value_key, low_id * total_panels + high_id)
        base = jax.random.normal(block_key, (BLOCK, BLOCK), jnp.float32)
        mirrored = (base + base.T) * 0.70710678
        chosen = jnp.where(diag, mirrored, jnp.where(flip, base.T, base))
        return (chosen * factor).astype(jnp.bfloat16)

    def one_member(entry):
        return jax.vmap(one_block)(entry)
    flat = (lower.reshape(MEMBERS, -1), upper.reshape(MEMBERS, -1), flipped.reshape(MEMBERS, -1), same.reshape(MEMBERS, -1))
    blocks = lax.map(one_member, flat)
    return blocks.reshape(MEMBERS, GROUPS, GROUPS, NNZ, BLOCK, BLOCK)


def levels(own_key, shape, cuts, smallest, top_value):
    factor_of = 1.0
    for dim, shards_of in cuts:
        heights = jax.random.uniform(jax.random.fold_in(jax.random.fold_in(own_key, 6), dim), (shards_of,), jnp.float32, smallest / len(cuts), top_value / len(cuts))
        factor_of = factor_of * jnp.repeat(jnp.exp(heights), shape[dim] // shards_of).reshape((-1,) + (1,) * (len(shape) - 1 - dim))
    return factor_of


def gaussian(key, shape, scale, most, cuts=(), kind=jnp.bfloat16):
    entries = scale * jax.random.normal(key, shape, jnp.float32)
    if cuts:
        entries = entries * levels(key, shape, cuts, -0.22, 0.18)
    return jnp.clip(entries, -most, most).astype(kind)


def setup_inputs(seed: int = 0) -> dict:
    key_list = jax.random.split(jax.random.key(seed), 7)
    features = gaussian(key_list[0], (NODES, WIDTH), 1.0, 6.0, ((0, 32),))
    weight = gaussian(key_list[1], (WIDTH, WIDTH), WIDTH ** -0.5, 0.375)
    bias = gaussian(key_list[2], (WIDTH,), 0.5, 3.0, (), jnp.float32)
    cotangent = gaussian(key_list[3], (NODES, WIDTH), 1.0, 6.0, ((0, 32),))
    adj_cols = draw_adj_cols(jax.random.fold_in(key_list[6], 71), 0)
    adj_vals = draw_adj_vals(jax.random.fold_in(key_list[6], 71), 0)
    return {"features": features, "weight": weight, "bias": bias, "cotangent": cotangent, "adj_cols": adj_cols, "adj_vals": adj_vals}


def forward_rows(adj_vals, adj_cols, source):
    block = adj_vals.shape[-1]
    width = source.shape[1]
    panels = source.reshape(GROUPS, MEMBERS, block, width)
    group_ids = jnp.arange(GROUPS, dtype=jnp.int32)

    def one_member(pair):
        columns, values = pair
        picked = panels[group_ids[None, :, None], columns]
        return jnp.einsum('rbkij,rbkjf->rif', values.astype(jnp.float32), picked.astype(jnp.float32))
    result = lax.map(one_member, (adj_cols, adj_vals))
    return jnp.transpose(result, (1, 0, 2, 3)).reshape(-1, width)

def backward_rows(adj_vals, adj_cols, source):
    block = adj_vals.shape[-1]
    width = source.shape[1]
    panels = source.reshape(GROUPS, MEMBERS, block, width).astype(jnp.float32)
    group_ids = jnp.arange(GROUPS, dtype=jnp.int32)

    def one_member(total, member):
        columns = adj_cols[member]
        values = adj_vals[member].astype(jnp.float32)
        rows_here = panels[:, member]
        contrib = jnp.einsum('rbkij,rif->rbkjf', values, rows_here)
        total = total.at[group_ids[None, :, None], columns].add(contrib)
        return (total, None)
    start = jnp.zeros((GROUPS, MEMBERS, block, width), jnp.float32)
    total, unused = lax.scan(one_member, start, jnp.arange(MEMBERS, dtype=jnp.int32))
    return total.reshape(-1, width)

def activation(value):
    return jax.nn.gelu(value, approximate=True)

def reference(features, weight, bias, cotangent, adj_cols, adj_vals):
    product = jnp.dot(features, weight, preferred_element_type=jnp.float32).astype(jnp.bfloat16)
    summed = forward_rows(adj_vals, adj_cols, product)
    pre = summed + bias.astype(jnp.float32)[None, :]
    activated, pullback = jax.vjp(activation, pre)
    hidden = activated.astype(jnp.bfloat16)
    pulled = pullback(cotangent.astype(jnp.float32))[0].astype(jnp.bfloat16)
    spread = backward_rows(adj_vals, adj_cols, pulled).astype(jnp.bfloat16)
    grad_input = jnp.dot(spread, weight.T, preferred_element_type=jnp.float32).astype(jnp.bfloat16)
    grad_weight = lax.dot_general(features, spread, (((0,), (0,)), ((), ())), preferred_element_type=jnp.float32)
    grad_bias = lax.optimization_barrier(jnp.sum(pulled.astype(jnp.float32), axis=0))
    return (hidden, grad_input, grad_weight, grad_bias)
```

```python
import functools

import jax
import jax.numpy as jnp
from jax import lax
from jax.experimental import pallas as pl
from jax.experimental.pallas import tpu as pltpu
from jax.sharding import PartitionSpec as P

PLANE = 4
MESH = pl.DeviceIdType.MESH


def flip(index, mask):
    bit = 1
    while bit <= mask:
        if mask & bit:
            index = index + bit - 2 * bit * ((index // bit) % 2)
        bit *= 2
    return index


def kernel(
    blks,
    team,
    rows,
    x_ref,
    w_ref,
    b_ref,
    ct_ref,
    cols_ref,
    vals_ref,
    hidden_ref,
    gi_ref,
    gw_ref,
    gb_ref,
    vals,
    dense,
    xbuf,
    pbuf,
    part,
    ybuf,
    sbuf,
    gpart,
    gl1,
    gtot,
    grs,
    gag,
    vals_sem,
    x_send,
    x_recv,
    p_send,
    p_recv,
    y_send,
    y_recv,
    s_send,
    s_recv,
    l1_send,
    l1_recv,
    rs_send,
    rs_recv,
    ag_send,
    ag_recv,
    l4_send,
    l4_recv,
):
    g = lax.axis_index("blk")
    m = lax.axis_index("team")
    block = x_ref.shape[0]
    width = x_ref.shape[1]
    nnz = vals_ref.shape[3]

    fetch = pltpu.make_async_copy(vals_ref, vals, vals_sem)
    fetch.start()

    barrier = pltpu.get_barrier_semaphore()
    for mask in range(1, team):
        pl.semaphore_signal(
            barrier, inc=1, device_id=(g, flip(m, mask)), device_id_type=MESH
        )
    for mask in range(1, blks):
        pl.semaphore_signal(
            barrier, inc=1, device_id=(flip(g, mask), m), device_id_type=MESH
        )

    def panel(buf, index):
        return buf.at[pl.ds(pl.multiple_of(index * block, block), block)]

    xbuf[pl.ds(pl.multiple_of(m * block, block), block), :] = x_ref[...]
    pl.semaphore_wait(barrier, team + blks - 2)

    pending = []

    def send(src, dst, send_sem, recv_sem, device):
        copy = pltpu.make_async_remote_copy(
            src_ref=src,
            dst_ref=dst,
            send_sem=send_sem,
            recv_sem=recv_sem,
            device_id=device,
            device_id_type=MESH,
        )
        copy.start()
        pending.append(copy)

    def arrived(dst, send_sem, recv_sem):
        pltpu.make_async_remote_copy(
            src_ref=dst,
            dst_ref=dst,
            send_sem=send_sem,
            recv_sem=recv_sem,
            device_id=(g, flip(m, 1)),
            device_id_type=MESH,
        ).wait_recv()

    def gather_open(buf, send_sems, recv_sems):
        own = panel(buf, m)
        for mask in range(PLANE, team, PLANE):
            send(own, own, send_sems.at[mask], recv_sems.at[mask], (g, flip(m, mask)))
        for mask in range(1, PLANE):
            send(own, own, send_sems.at[mask], recv_sems.at[mask], (g, flip(m, mask)))

    def gather_forward(buf, send_sems, recv_sems):
        for far in range(PLANE, team, PLANE):
            item = panel(buf, flip(m, far))
            arrived(item, send_sems.at[far], recv_sems.at[far])
            for near in range(1, PLANE):
                send(
                    item,
                    item,
                    send_sems.at[far + near],
                    recv_sems.at[far + near],
                    (g, flip(m, near)),
                )

    def gather_close(buf, send_sems, recv_sems):
        for far in range(0, team, PLANE):
            for near in range(1, PLANE):
                mask = far + near
                arrived(panel(buf, flip(m, mask)), send_sems.at[mask], recv_sems.at[mask])

    def exchange(src_of, buf, send_sems, recv_sems):
        for mask in range(1, blks):
            peer = flip(g, mask)
            send(src_of(peer), buf.at[g], send_sems.at[mask], recv_sems.at[mask], (peer, m))

    def exchanged(buf, send_sems, recv_sems):
        for mask in range(1, blks):
            arrived(buf.at[flip(g, mask)], send_sems.at[mask], recv_sems.at[mask])

    tall = min(2, blks) * block
    deep = min(8, team) * block

    def aggregate(buf):
        for top in range(0, blks * block, tall):
            if team * block == 2 * deep:
                total = jnp.dot(
                    dense[top : top + tall, :deep],
                    buf[:deep, :],
                    preferred_element_type=jnp.float32,
                )
                part[top : top + tall, :] = total + jnp.dot(
                    dense[top : top + tall, deep:],
                    buf[deep:, :],
                    preferred_element_type=jnp.float32,
                )
            else:
                part[top : top + tall, :] = jnp.zeros((tall, width), jnp.float32)

                def step(i, carry, top=top):
                    span = pl.ds(pl.multiple_of(i * deep, deep), deep)
                    part[top : top + tall, :] += jnp.dot(
                        dense[top : top + tall, span],
                        buf[span, :],
                        preferred_element_type=jnp.float32,
                    )
                    return carry

                lax.fori_loop(0, team * block // deep, step, 0)

    def part_of(peer):
        return panel(part, peer)

    def own_part():
        return part[pl.ds(pl.multiple_of(g * block, block), block), :]

    gather_open(xbuf, x_send, x_recv)
    fetch.wait()

    def lay(c, carry):
        for r in range(blks):
            slot = 0
            found = 0
            for k in range(nnz):
                hit = cols_ref[0, r, 0, k] == c
                slot = jnp.where(hit, k, slot)
                found = jnp.where(hit, 1, found)
            keep = found.astype(jnp.float32)
            item = vals[0, r, 0, slot].astype(jnp.float32) * keep
            span = pl.ds(pl.multiple_of(c * block, block), block)
            dense[r * block : (r + 1) * block, span] = item.astype(jnp.bfloat16)
        return carry

    third = team // PLANE
    lax.fori_loop(0, third, lay, 0)
    gather_forward(xbuf, x_send, x_recv)
    lax.fori_loop(third, team, lay, 0)
    gather_close(xbuf, x_send, x_recv)
    aggregate(xbuf)
    first = len(pending)
    exchange(part_of, ybuf, y_send, y_recv)
    parted = pending[first:]
    del pending[first:]
    y = own_part()
    exchanged(ybuf, y_send, y_recv)
    for mask in range(1, blks):
        y = y + ybuf[flip(g, mask)]
    high = y.astype(jnp.bfloat16)
    low = (y - high.astype(jnp.float32)).astype(jnp.bfloat16)
    weight = w_ref[...]
    pre = (
        jnp.dot(high, weight, preferred_element_type=jnp.float32)
        + jnp.dot(low, weight, preferred_element_type=jnp.float32)
        + b_ref[...]
    )
    square = pre * pre
    bent = jnp.tanh(0.7978845608 * (pre + 0.044715 * (square * pre)))
    half = 0.5 * (1.0 + bent)
    slope = half + (0.5 * pre) * ((1.0 - bent) * (1.0 + bent)) * (
        0.7978845608 * (1.0 + 0.134145 * square)
    )
    pulled = (ct_ref[...].astype(jnp.float32) * slope).astype(jnp.bfloat16)

    pbuf[pl.ds(pl.multiple_of(m * block, block), block), :] = pulled
    gather_open(pbuf, p_send, p_recv)
    hidden_ref[...] = (pre * half).astype(jnp.bfloat16)

    turned = (((0,), (0,)), ((), ()))
    grad = lax.dot_general(high, pulled, turned, preferred_element_type=jnp.float32)
    grad = grad + lax.dot_general(low, pulled, turned, preferred_element_type=jnp.float32)
    count = grad.shape[0] // rows
    chunks = blks * team
    if count < chunks:
        gpart[count:, :, :width] = jnp.zeros((chunks - count, rows, width), jnp.float32)
    gpart[:count, :, :width] = grad.reshape(count, rows, width)
    column = jnp.sum(pulled.astype(jnp.float32), axis=0, keepdims=True)
    lanes = width // 2
    line = lax.broadcasted_iota(jnp.int32, (rows, lanes), 0)
    tail = jnp.where(
        line == 0,
        jnp.broadcast_to(column[:, :lanes], (rows, lanes)),
        jnp.where(line == 1, jnp.broadcast_to(column[:, lanes:], (rows, lanes)), 0.0),
    )
    gpart[:, :, width:] = jnp.broadcast_to(tail[None], (chunks, rows, lanes))
    exchange(lambda peer: gpart.at[pl.ds(peer * team, team)], gl1, l1_send, l1_recv)

    gather_forward(pbuf, p_send, p_recv)

    exchanged(gl1, l1_send, l1_recv)
    total = gpart[pl.ds(g * team, team)]
    for mask in range(1, blks):
        total = total + gl1[flip(g, mask)]
    gtot[...] = total
    for mask in range(1, team):
        peer = flip(m, mask)
        send(gtot.at[peer], grs.at[m], rs_send.at[mask], rs_recv.at[mask], (g, peer))
    grs[m] = gtot[m]
    for mask in range(1, team):
        arrived(grs.at[flip(m, mask)], rs_send.at[mask], rs_recv.at[mask])
    mine = jnp.sum(grs[...], axis=0)
    gag[g, m] = mine[:, :width]
    gb_ref[:, :lanes] = mine[0:1, width:]
    gb_ref[:, lanes:] = mine[1:2, width:]
    for mask in range(1, team):
        send(
            gag.at[g, m],
            gag.at[g, m],
            ag_send.at[mask],
            ag_recv.at[mask],
            (g, flip(m, mask)),
        )

    gather_close(pbuf, p_send, p_recv)
    for copy in parted:
        copy.wait_send()
    aggregate(pbuf)
    exchange(part_of, sbuf, s_send, s_recv)
    for mask in range(1, team):
        arrived(gag.at[g, flip(m, mask)], ag_send.at[mask], ag_recv.at[mask])
    exchange(lambda peer: gag.at[g], gag, l4_send, l4_recv)
    spread = own_part()
    exchanged(sbuf, s_send, s_recv)
    for mask in range(1, blks):
        spread = spread + sbuf[flip(g, mask)]
    gi_ref[...] = lax.dot_general(
        spread.astype(jnp.bfloat16),
        weight,
        (((1,), (1,)), ((), ())),
        preferred_element_type=jnp.float32,
    ).astype(jnp.bfloat16)
    exchanged(gag, l4_send, l4_recv)
    gw_ref[...] = gag[...].reshape(chunks * rows, width)[: gw_ref.shape[0]]
    for copy in pending:
        copy.wait_send()


def local(blks, team, features, weight, bias, cotangent, adj_cols, adj_vals):
    block, width = features.shape
    rows = 8 * pl.cdiv(width, 8 * blks * team)
    wide = width + width // 2
    f32, bf16 = jnp.float32, jnp.bfloat16
    dma = pltpu.SemaphoreType.DMA
    vmem = pl.BlockSpec(memory_space=pltpu.VMEM)
    panels = blks * block
    hidden, grad_input, grad_weight, grad_bias = pl.pallas_call(
        functools.partial(kernel, blks, team, rows),
        out_shape=(
            jax.ShapeDtypeStruct((block, width), bf16),
            jax.ShapeDtypeStruct((block, width), bf16),
            jax.ShapeDtypeStruct((width, width), f32),
            jax.ShapeDtypeStruct((1, width), f32),
        ),
        in_specs=[
            vmem,
            vmem,
            vmem,
            vmem,
            pl.BlockSpec(memory_space=pltpu.SMEM),
            pl.BlockSpec(memory_space=pl.ANY),
        ],
        out_specs=(vmem, vmem, vmem, vmem),
        scratch_shapes=[
            pltpu.VMEM(adj_vals.shape, bf16),
            pltpu.VMEM((panels, team * block), bf16),
            pltpu.VMEM((team * block, width), bf16),
            pltpu.VMEM((team * block, width), bf16),
            pltpu.VMEM((panels, width), f32),
            pltpu.VMEM((blks, block, width), f32),
            pltpu.VMEM((blks, block, width), f32),
            pltpu.VMEM((blks * team, rows, wide), f32),
            pltpu.VMEM((blks, team, rows, wide), f32),
            pltpu.VMEM((team, rows, wide), f32),
            pltpu.VMEM((team, rows, wide), f32),
            pltpu.VMEM((blks, team, rows, width), f32),
            dma,
            dma((team,)),
            dma((team,)),
            dma((team,)),
            dma((team,)),
            dma((blks,)),
            dma((blks,)),
            dma((blks,)),
            dma((blks,)),
            dma((blks,)),
            dma((blks,)),
            dma((team,)),
            dma((team,)),
            dma((team,)),
            dma((team,)),
            dma((blks,)),
            dma((blks,)),
        ],
        compiler_params=pltpu.CompilerParams(
            collective_id=0, has_side_effects=True, vmem_limit_bytes=56 * 2**20
        ),
    )(features, weight, bias.reshape(1, width), cotangent, adj_cols, adj_vals)
    return hidden, grad_input, grad_weight, grad_bias.reshape(width)


def solution(mesh):
    return jax.shard_map(
        functools.partial(local, mesh.shape["blk"], mesh.shape["team"]),
        mesh=mesh,
        in_specs=(
            P(("blk", "team"), None),
            P(),
            P(),
            P(("blk", "team"), None),
            P("team", None, "blk", None),
            P("team", None, "blk", None, None, None),
        ),
        out_specs=(P(("blk", "team"), None), P(("blk", "team"), None), P(), P()),
        check_vma=False,
    )
```

```python
import functools
import math

import jax
import jax.numpy as jnp
from jax import lax
from jax.experimental import pallas as pl
from jax.experimental.pallas import tpu as pltpu
from jax.sharding import PartitionSpec as P

PLANE = 4
MESH = pl.DeviceIdType.MESH


def flip(index, mask):
    bit = 1
    while bit <= mask:
        if mask & bit:
            index = index + bit - 2 * bit * ((index // bit) % 2)
        bit *= 2
    return index


def kernel(
    blks,
    team,
    x_ref,
    w_ref,
    b_ref,
    ct_ref,
    cols_ref,
    vals_ref,
    hidden_ref,
    gi_ref,
    gw_ref,
    gb_ref,
    vals,
    dense,
    xbuf,
    pbuf,
    part,
    back,
    ybuf,
    sbuf,
    gpart,
    gl1,
    gtot,
    gplane,
    gsum,
    gline,
    gag,
    vals_sem,
    x_send,
    x_recv,
    x_send2,
    x_recv2,
    p_send,
    p_recv,
    p_send2,
    p_recv2,
    y_send,
    y_recv,
    s_send,
    s_recv,
    l1_send,
    l1_recv,
    rs_send,
    rs_recv,
    ag_send,
    ag_recv,
    l4_send,
    l4_recv,
):
    g = lax.axis_index("blk")
    m = lax.axis_index("team")
    block = x_ref.shape[0]
    width = x_ref.shape[1]
    nnz = vals_ref.shape[3]
    line = team // PLANE
    z, p = m // PLANE, m % PLANE
    half = block // 2
    fars = list(range(PLANE, team, PLANE))

    fetch = pltpu.make_async_copy(vals_ref, vals, vals_sem)
    fetch.start()

    barrier = pltpu.get_barrier_semaphore()
    partners = list(range(1, PLANE)) + fars
    for mask in partners:
        pl.semaphore_signal(
            barrier, inc=1, device_id=(g, flip(m, mask)), device_id_type=MESH
        )
    for mask in range(1, blks):
        pl.semaphore_signal(
            barrier, inc=1, device_id=(flip(g, mask), m), device_id_type=MESH
        )

    def rows_of(index, start=0, size=block):
        return pl.ds(pl.multiple_of(index * block + start, half), size)

    xbuf[rows_of(m), :] = x_ref[...]
    fetch.wait()

    def lay(c, carry):
        for r in range(blks):
            slot = 0
            found = 0
            for k in range(nnz):
                hit = cols_ref[0, r, 0, k] == c
                slot = jnp.where(hit, k, slot)
                found = jnp.where(hit, 1, found)
            keep = found.astype(jnp.float32)
            item = vals[0, r, 0, slot].astype(jnp.float32) * keep
            span = pl.ds(pl.multiple_of(c * block, block), block)
            dense[r * block : (r + 1) * block, span] = item.astype(jnp.bfloat16)
        return carry

    lax.fori_loop(0, team // 4, lay, 0)
    dense[blks * block :, :] = jnp.ones((16, team * block), jnp.bfloat16)
    pl.semaphore_wait(barrier, len(partners) + blks - 1)

    pending = []

    def send(src, dst, send_sem, recv_sem, device):
        copy = pltpu.make_async_remote_copy(
            src_ref=src,
            dst_ref=dst,
            send_sem=send_sem,
            recv_sem=recv_sem,
            device_id=device,
            device_id_type=MESH,
        )
        copy.start()
        pending.append(copy)

    def arrived(dst, send_sem, recv_sem):
        pltpu.make_async_remote_copy(
            src_ref=dst,
            dst_ref=dst,
            send_sem=send_sem,
            recv_sem=recv_sem,
            device_id=(g, flip(m, 1)),
            device_id_type=MESH,
        ).wait_recv()

    class Gather:
        def __init__(self, buf, sends, recvs, sends2, recvs2):
            self.buf = buf
            self.sems = (sends, recvs)
            self.sems2 = (sends2, recvs2)

        def item(self, mask):
            return self.buf.at[rows_of(flip(m, mask))]

        def spread(self, far):
            for near in (1, 2):
                item = self.item(far)
                sends, recvs = self.sems
                send(item, item, sends.at[far + near], recvs.at[far + near], (g, flip(m, near)))

        def open(self):
            self.spread(0)
            sends, recvs = self.sems
            for far in fars:
                item = self.item(0)
                send(item, item, sends.at[far], recvs.at[far], (g, flip(m, far)))

        def wait(self, mask):
            sends, recvs = self.sems
            arrived(self.item(mask), sends.at[mask], recvs.at[mask])

        def forward(self, far):
            self.wait(far)
            self.spread(far)

        def cross(self, far):
            for near, sems, start in ((1, self.sems, 0), (2, self.sems2, half)):
                self.wait(far + near)
                item = self.buf.at[rows_of(flip(m, far + near), start, half)]
                mask = far + 3
                send(item, item, sems[0].at[mask], sems[1].at[mask], (g, flip(m, 3 - near)))

        def close(self):
            for far in [0] + fars:
                mask = far + 3
                for sems, start in ((self.sems, 0), (self.sems2, half)):
                    item = self.buf.at[rows_of(flip(m, mask), start, half)]
                    arrived(item, sems[0].at[mask], sems[1].at[mask])

    def exchange(src_of, buf, send_sems, recv_sems):
        for mask in range(1, blks):
            peer = flip(g, mask)
            send(src_of(peer), buf.at[g], send_sems.at[mask], recv_sems.at[mask], (peer, m))

    def exchanged(buf, send_sems, recv_sems):
        for mask in range(1, blks):
            arrived(buf.at[flip(g, mask)], send_sems.at[mask], recv_sems.at[mask])

    deep = min(8, team) * block

    def aggregate(buf, top, tall):
        def term(span):
            return jnp.dot(
                dense[top : top + tall, span],
                buf[span, :],
                preferred_element_type=jnp.float32,
            )

        if team * block <= 2 * deep:
            return sum(term(slice(i, i + deep)) for i in range(0, team * block, deep))

        def step(i, total):
            return total + term(pl.ds(pl.multiple_of(i * deep, deep), deep))

        start = jnp.zeros((tall, width), jnp.float32)
        return lax.fori_loop(0, team * block // deep, step, start)

    tall = min(2, blks) * block

    xs = Gather(xbuf, x_send, x_recv, x_send2, x_recv2)
    xs.open()
    lax.fori_loop(team // 4, team // 2, lay, 0)
    for place, far in enumerate(fars):
        xs.forward(far)
        xs.cross(far - PLANE)
    lax.fori_loop(team // 2, team, lay, 0)
    xs.cross(fars[-1])
    xs.close()
    for top in range(0, blks * block, tall):
        part[pl.ds(top // block, tall // block)] = aggregate(xbuf, top, tall).reshape(
            tall // block, block, width
        )
    exchange(lambda peer: part.at[peer], ybuf, y_send, y_recv)
    y = part[g]
    exchanged(ybuf, y_send, y_recv)
    for mask in range(1, blks):
        y = y + ybuf[flip(g, mask)]
    high = y.astype(jnp.bfloat16)
    low = (y - high.astype(jnp.float32)).astype(jnp.bfloat16)
    weight = w_ref[...]
    pre = (
        jnp.dot(high, weight, preferred_element_type=jnp.float32)
        + jnp.dot(low, weight, preferred_element_type=jnp.float32)
        + b_ref[...]
    )
    square = pre * pre
    bent = jnp.tanh(0.7978845608 * (pre + 0.044715 * (square * pre)))
    gate = 0.5 * (1.0 + bent)
    slope = gate + (0.5 * pre) * ((1.0 - bent) * (1.0 + bent)) * (
        0.7978845608 * (1.0 + 0.134145 * square)
    )
    pulled = (ct_ref[...].astype(jnp.float32) * slope).astype(jnp.bfloat16)

    pbuf[rows_of(m), :] = pulled
    ps = Gather(pbuf, p_send, p_recv, p_send2, p_recv2)
    ps.open()
    turned = (((0,), (0,)), ((), ()))
    grad = lax.dot_general(high, pulled, turned, preferred_element_type=jnp.float32)
    grad = grad + lax.dot_general(low, pulled, turned, preferred_element_type=jnp.float32)
    chunk = gpart.shape[3]
    count = width // chunk
    chunks = blks * team
    whole = grad.reshape(count, chunk, width)
    if count < chunks:
        empty = jnp.zeros((chunks - count, chunk, width), jnp.float32)
        whole = jnp.concatenate([whole, empty], axis=0)
    gpart[...] = whole.reshape(blks, PLANE, line, chunk, width)
    exchange(lambda peer: gpart.at[peer], gl1, l1_send, l1_recv)
    hidden_ref[...] = (pre * gate).astype(jnp.bfloat16)

    ps.forward(fars[0])
    ps.cross(0)

    exchanged(gl1, l1_send, l1_recv)
    total = gpart[g]
    for mask in range(1, blks):
        total = total + gl1[flip(g, mask)]
    gtot[...] = total
    for near in range(1, PLANE):
        send(
            gtot.at[flip(p, near)],
            gplane.at[p],
            rs_send.at[near],
            rs_recv.at[near],
            (g, flip(m, near)),
        )
    gplane[p] = gtot[p]

    for far in fars[1:]:
        ps.forward(far)
        ps.cross(far - PLANE)
    for near in range(1, PLANE):
        arrived(gplane.at[flip(p, near)], rs_send.at[near], rs_recv.at[near])
    gsum[...] = jnp.sum(gplane[...], axis=0)
    for far in fars:
        send(
            gsum.at[flip(z, far // PLANE)],
            gline.at[z],
            rs_send.at[far],
            rs_recv.at[far],
            (g, flip(m, far)),
        )
    gline[z] = gsum[z]
    ps.cross(fars[-1])
    for far in fars:
        arrived(gline.at[flip(z, far // PLANE)], rs_send.at[far], rs_recv.at[far])
    gag[g, z, p] = jnp.sum(gline[...], axis=0)
    for near in range(1, PLANE):
        item = gag.at[g, z, p]
        send(item, item, ag_send.at[near], ag_recv.at[near], (g, flip(m, near)))
    ps.close()
    for top in range(0, blks * block, tall):
        extra = 16 if top + tall == blks * block else 0
        total = aggregate(pbuf, top, tall + extra)
        back[pl.ds(top // block, tall // block), :block] = total[:tall].reshape(
            tall // block, block, width
        )
    for r in range(blks):
        back[r, block:] = total[tall : tall + 8]
    exchange(lambda peer: back.at[peer], sbuf, s_send, s_recv)
    for near in range(1, PLANE):
        arrived(gag.at[g, z, flip(p, near)], ag_send.at[near], ag_recv.at[near])
    for far in fars:
        item = gag.at[g, z]
        send(item, item, ag_send.at[far], ag_recv.at[far], (g, flip(m, far)))
    spread = back[g]
    exchanged(sbuf, s_send, s_recv)
    for mask in range(1, blks):
        spread = spread + sbuf[flip(g, mask)]
    gi_ref[...] = lax.dot_general(
        spread[:block].astype(jnp.bfloat16),
        weight,
        (((1,), (1,)), ((), ())),
        preferred_element_type=jnp.float32,
    ).astype(jnp.bfloat16)
    gb_ref[...] = spread[block : block + 1]
    for far in fars:
        arrived(gag.at[g, flip(z, far // PLANE)], ag_send.at[far], ag_recv.at[far])
    exchange(lambda peer: gag.at[g], gag, l4_send, l4_recv)
    exchanged(gag, l4_send, l4_recv)
    for i in range(count):
        b, q, l = i // team, i // line % PLANE, i % line
        gw_ref[i * chunk : (i + 1) * chunk] = gag[b, l, q]
    for copy in pending:
        copy.wait_send()


def hand_out(*refs):
    count = len(refs) // 2
    sems = refs[-1]
    copies = [
        pltpu.make_async_copy(refs[i], refs[count + i], sems.at[i]) for i in range(count)
    ]
    for copy in copies:
        copy.start()
    for copy in copies:
        copy.wait()


def local(blks, team, features, weight, bias, cotangent, adj_cols, adj_vals):
    block, width = features.shape
    line = team // PLANE
    chunk = 8 * pl.cdiv(width, 8 * blks * team)
    f32, bf16 = jnp.float32, jnp.bfloat16
    dma = pltpu.SemaphoreType.DMA
    vmem = pl.BlockSpec(memory_space=pltpu.VMEM)
    anywhere = pl.BlockSpec(memory_space=pl.ANY)
    panels = blks * block
    outs = (
        jax.ShapeDtypeStruct((block, width), bf16),
        jax.ShapeDtypeStruct((block, width), bf16),
        jax.ShapeDtypeStruct((width, width), f32),
        jax.ShapeDtypeStruct((1, width), f32),
    )
    buffers = [
        (adj_vals.shape, bf16),
        ((panels + 16, team * block), bf16),
        ((team * block, width), bf16),
        ((team * block, width), bf16),
        ((blks, block, width), f32),
        ((blks, block + 8, width), f32),
        ((blks, block, width), f32),
        ((blks, block + 8, width), f32),
        ((blks, PLANE, line, chunk, width), f32),
        ((blks, PLANE, line, chunk, width), f32),
        ((PLANE, line, chunk, width), f32),
        ((PLANE, line, chunk, width), f32),
        ((line, chunk, width), f32),
        ((line, chunk, width), f32),
        ((blks, line, PLANE, chunk, width), f32),
    ]
    held = sum(math.prod(shape) * jnp.dtype(kind).itemsize for shape, kind in buffers)
    results = pl.pallas_call(
        functools.partial(kernel, blks, team),
        out_shape=outs,
        in_specs=[vmem, vmem, vmem, vmem, pl.BlockSpec(memory_space=pltpu.SMEM), anywhere],
        out_specs=(vmem,) * 4,
        scratch_shapes=[pltpu.VMEM(shape, kind) for shape, kind in buffers]
        + [dma]
        + [dma((team,))] * 8
        + [dma((blks,))] * 6
        + [dma((team,))] * 4
        + [dma((blks,))] * 2,
        compiler_params=pltpu.CompilerParams(
            collective_id=0, has_side_effects=True, vmem_limit_bytes=held + 12 * 2**20
        ),
    )(features, weight, bias.reshape(1, width), cotangent, adj_cols, adj_vals)
    hidden, grad_input, grad_weight, grad_bias = pl.pallas_call(
        hand_out,
        out_shape=outs,
        in_specs=[anywhere] * 4,
        out_specs=(anywhere,) * 4,
        scratch_shapes=[dma((4,))],
    )(*results)
    return hidden, grad_input, grad_weight, grad_bias.reshape(width)


def solution(mesh):
    return jax.shard_map(
        functools.partial(local, mesh.shape["blk"], mesh.shape["team"]),
        mesh=mesh,
        in_specs=(
            P(("blk", "team"), None),
            P(),
            P(),
            P(("blk", "team"), None),
            P("team", None, "blk", None),
            P("team", None, "blk", None, None, None),
        ),
        out_specs=(P(("blk", "team"), None), P(("blk", "team"), None), P(), P()),
        check_vma=False,
    )
```

```python
import functools

import jax
import jax.numpy as jnp
from jax import lax
from jax.experimental import pallas as pl
from jax.experimental.pallas import tpu as pltpu
from jax.sharding import PartitionSpec as P

PLANE = 4
MESH = pl.DeviceIdType.MESH


def flip(index, mask):
    bit = 1
    while bit <= mask:
        if mask & bit:
            index = index + bit - 2 * bit * ((index // bit) % 2)
        bit *= 2
    return index


def kernel(
    blks,
    team,
    x_ref,
    w_ref,
    b_ref,
    ct_ref,
    cols_ref,
    vals_ref,
    hidden_ref,
    gi_ref,
    gw_ref,
    gb_ref,
    vals,
    dense,
    xbuf,
    pbuf,
    part,
    back,
    ybuf,
    sbuf,
    gpart,
    gl1,
    gtot,
    grs,
    gag,
    vals_sem,
    x_send,
    x_recv,
    x_send2,
    x_recv2,
    p_send,
    p_recv,
    p_send2,
    p_recv2,
    y_send,
    y_recv,
    s_send,
    s_recv,
    l1_send,
    l1_recv,
    rs_send,
    rs_recv,
    ag_send,
    ag_recv,
    l4_send,
    l4_recv,
):
    g = lax.axis_index("blk")
    m = lax.axis_index("team")
    block = x_ref.shape[0]
    width = x_ref.shape[1]
    nnz = vals_ref.shape[3]
    half = block // 2
    fars = list(range(PLANE, team, PLANE))

    fetch = pltpu.make_async_copy(vals_ref, vals, vals_sem)
    fetch.start()

    barrier = pltpu.get_barrier_semaphore()
    partners = list(range(1, PLANE)) + fars
    for mask in partners:
        pl.semaphore_signal(
            barrier, inc=1, device_id=(g, flip(m, mask)), device_id_type=MESH
        )
    for mask in range(1, blks):
        pl.semaphore_signal(
            barrier, inc=1, device_id=(flip(g, mask), m), device_id_type=MESH
        )

    def rows_of(index, start=0, size=block):
        return pl.ds(pl.multiple_of(index * block + start, half), size)

    xbuf[rows_of(m), :] = x_ref[...]
    fetch.wait()

    def lay(c, carry):
        for r in range(blks):
            slot = 0
            found = 0
            for k in range(nnz):
                hit = cols_ref[0, r, 0, k] == c
                slot = jnp.where(hit, k, slot)
                found = jnp.where(hit, 1, found)
            keep = found.astype(jnp.float32)
            item = vals[0, r, 0, slot].astype(jnp.float32) * keep
            span = pl.ds(pl.multiple_of(c * block, block), block)
            dense[r * block : (r + 1) * block, span] = item.astype(jnp.bfloat16)
        return carry

    lax.fori_loop(0, team // 4, lay, 0)
    dense[blks * block :, :] = jnp.ones((16, team * block), jnp.bfloat16)
    pl.semaphore_wait(barrier, len(partners) + blks - 1)

    pending = []

    def send(src, dst, send_sem, recv_sem, device):
        copy = pltpu.make_async_remote_copy(
            src_ref=src,
            dst_ref=dst,
            send_sem=send_sem,
            recv_sem=recv_sem,
            device_id=device,
            device_id_type=MESH,
        )
        copy.start()
        pending.append(copy)

    def arrived(dst, send_sem, recv_sem):
        pltpu.make_async_remote_copy(
            src_ref=dst,
            dst_ref=dst,
            send_sem=send_sem,
            recv_sem=recv_sem,
            device_id=(g, flip(m, 1)),
            device_id_type=MESH,
        ).wait_recv()

    class Gather:
        def __init__(self, buf, sends, recvs, sends2, recvs2):
            self.buf = buf
            self.sems = (sends, recvs)
            self.sems2 = (sends2, recvs2)

        def item(self, mask):
            return self.buf.at[rows_of(flip(m, mask))]

        def spread(self, far):
            for near in (1, 2):
                item = self.item(far)
                sends, recvs = self.sems
                send(item, item, sends.at[far + near], recvs.at[far + near], (g, flip(m, near)))

        def open(self):
            self.spread(0)
            sends, recvs = self.sems
            for far in fars:
                item = self.item(0)
                send(item, item, sends.at[far], recvs.at[far], (g, flip(m, far)))

        def wait(self, mask):
            sends, recvs = self.sems
            arrived(self.item(mask), sends.at[mask], recvs.at[mask])

        def forward(self, far):
            self.wait(far)
            self.spread(far)

        def cross(self, far):
            for near, sems, start in ((1, self.sems, 0), (2, self.sems2, half)):
                self.wait(far + near)
                item = self.buf.at[rows_of(flip(m, far + near), start, half)]
                mask = far + 3
                send(item, item, sems[0].at[mask], sems[1].at[mask], (g, flip(m, 3 - near)))

        def close(self):
            for far in [0] + fars:
                mask = far + 3
                for sems, start in ((self.sems, 0), (self.sems2, half)):
                    item = self.buf.at[rows_of(flip(m, mask), start, half)]
                    arrived(item, sems[0].at[mask], sems[1].at[mask])

    def exchange(src_of, buf, send_sems, recv_sems):
        for mask in range(1, blks):
            peer = flip(g, mask)
            send(src_of(peer), buf.at[g], send_sems.at[mask], recv_sems.at[mask], (peer, m))

    def exchanged(buf, send_sems, recv_sems):
        for mask in range(1, blks):
            arrived(buf.at[flip(g, mask)], send_sems.at[mask], recv_sems.at[mask])

    deep = min(8, team) * block

    def aggregate(buf, top, tall):
        def term(span):
            return jnp.dot(
                dense[top : top + tall, span],
                buf[span, :],
                preferred_element_type=jnp.float32,
            )

        if team * block <= 2 * deep:
            return sum(term(slice(i, i + deep)) for i in range(0, team * block, deep))

        def step(i, total):
            return total + term(pl.ds(pl.multiple_of(i * deep, deep), deep))

        start = jnp.zeros((tall, width), jnp.float32)
        return lax.fori_loop(0, team * block // deep, step, start)

    tall = min(2, blks) * block

    xs = Gather(xbuf, x_send, x_recv, x_send2, x_recv2)
    xs.open()
    lax.fori_loop(team // 4, team // 2, lay, 0)
    for place, far in enumerate(fars):
        xs.forward(far)
        xs.cross(far - PLANE)
    lax.fori_loop(team // 2, team, lay, 0)
    xs.cross(fars[-1])
    xs.close()
    for top in range(0, blks * block, tall):
        part[pl.ds(top // block, tall // block)] = aggregate(xbuf, top, tall).reshape(
            tall // block, block, width
        )
    exchange(lambda peer: part.at[peer], ybuf, y_send, y_recv)
    y = part[g]
    exchanged(ybuf, y_send, y_recv)
    for mask in range(1, blks):
        y = y + ybuf[flip(g, mask)]
    high = y.astype(jnp.bfloat16)
    low = (y - high.astype(jnp.float32)).astype(jnp.bfloat16)
    weight = w_ref[...]
    pre = (
        jnp.dot(high, weight, preferred_element_type=jnp.float32)
        + jnp.dot(low, weight, preferred_element_type=jnp.float32)
        + b_ref[...]
    )
    square = pre * pre
    bent = jnp.tanh(0.7978845608 * (pre + 0.044715 * (square * pre)))
    gate = 0.5 * (1.0 + bent)
    slope = gate + (0.5 * pre) * ((1.0 - bent) * (1.0 + bent)) * (
        0.7978845608 * (1.0 + 0.134145 * square)
    )
    pulled = (ct_ref[...].astype(jnp.float32) * slope).astype(jnp.bfloat16)

    pbuf[rows_of(m), :] = pulled
    ps = Gather(pbuf, p_send, p_recv, p_send2, p_recv2)
    ps.open()
    turned = (((0,), (0,)), ((), ()))
    grad = lax.dot_general(high, pulled, turned, preferred_element_type=jnp.float32)
    grad = grad + lax.dot_general(low, pulled, turned, preferred_element_type=jnp.float32)
    chunk = gpart.shape[2]
    count = width // chunk
    chunks = blks * team
    whole = grad.reshape(count, chunk, width)
    if count < chunks:
        empty = jnp.zeros((chunks - count, chunk, width), jnp.float32)
        whole = jnp.concatenate([whole, empty], axis=0)
    gpart[...] = whole.reshape(blks, team, chunk, width)
    exchange(lambda peer: gpart.at[peer], gl1, l1_send, l1_recv)
    ps.forward(fars[0])

    exchanged(gl1, l1_send, l1_recv)
    total = gpart[g]
    for mask in range(1, blks):
        total = total + gl1[flip(g, mask)]
    gtot[...] = total
    for mask in range(1, team):
        peer = flip(m, mask)
        send(gtot.at[peer], grs.at[m], rs_send.at[mask], rs_recv.at[mask], (g, peer))
    grs[m] = gtot[m]
    hidden_ref[...] = (pre * gate).astype(jnp.bfloat16)

    ps.cross(0)
    for far in fars[1:]:
        ps.forward(far)
        ps.cross(far - PLANE)
    for mask in range(1, team):
        arrived(grs.at[flip(m, mask)], rs_send.at[mask], rs_recv.at[mask])
    gag[g, m] = jnp.sum(grs[...], axis=0)
    for mask in range(1, team):
        item = gag.at[g, m]
        send(item, item, ag_send.at[mask], ag_recv.at[mask], (g, flip(m, mask)))
    ps.cross(fars[-1])
    ps.close()
    for top in range(0, blks * block, tall):
        extra = 16 if top + tall == blks * block else 0
        total = aggregate(pbuf, top, tall + extra)
        back[pl.ds(top // block, tall // block), :block] = total[:tall].reshape(
            tall // block, block, width
        )
    for r in range(blks):
        back[r, block:] = total[tall : tall + 8]
    exchange(lambda peer: back.at[peer], sbuf, s_send, s_recv)
    for mask in range(1, team):
        arrived(gag.at[g, flip(m, mask)], ag_send.at[mask], ag_recv.at[mask])
    exchange(lambda peer: gag.at[g], gag, l4_send, l4_recv)
    spread = back[g]
    exchanged(sbuf, s_send, s_recv)
    for mask in range(1, blks):
        spread = spread + sbuf[flip(g, mask)]
    gi_ref[...] = lax.dot_general(
        spread[:block].astype(jnp.bfloat16),
        weight,
        (((1,), (1,)), ((), ())),
        preferred_element_type=jnp.float32,
    ).astype(jnp.bfloat16)
    gb_ref[...] = spread[block : block + 1]
    exchanged(gag, l4_send, l4_recv)
    gw_ref[...] = gag[...].reshape(chunks * chunk, width)[:width]
    for copy in pending:
        copy.wait_send()


def hand_out(*refs):
    count = len(refs) // 3
    takes, gives, slots, (into, out) = (
        refs[:count],
        refs[count : 2 * count],
        refs[2 * count : 3 * count],
        refs[3 * count :],
    )
    first = [pltpu.make_async_copy(takes[i], slots[i], into.at[i]) for i in range(count)]
    second = [pltpu.make_async_copy(slots[i], gives[i], out.at[i]) for i in range(count)]
    for copy in first:
        copy.start()
    for copy, onward in zip(first, second):
        copy.wait()
        onward.start()
    for copy in second:
        copy.wait()


def local(blks, team, features, weight, bias, cotangent, adj_cols, adj_vals):
    block, width = features.shape
    chunk = 8 * pl.cdiv(width, 8 * blks * team)
    f32, bf16 = jnp.float32, jnp.bfloat16
    dma = pltpu.SemaphoreType.DMA
    vmem = pl.BlockSpec(memory_space=pltpu.VMEM)
    anywhere = pl.BlockSpec(memory_space=pl.ANY)
    panels = blks * block
    outs = (
        jax.ShapeDtypeStruct((block, width), bf16),
        jax.ShapeDtypeStruct((block, width), bf16),
        jax.ShapeDtypeStruct((width, width), f32),
        jax.ShapeDtypeStruct((1, width), f32),
    )
    buffers = [
        (adj_vals.shape, bf16),
        ((panels + 16, team * block), bf16),
        ((team * block, width), bf16),
        ((team * block, width), bf16),
        ((blks, block, width), f32),
        ((blks, block + 8, width), f32),
        ((blks, block, width), f32),
        ((blks, block + 8, width), f32),
        ((blks, team, chunk, width), f32),
        ((blks, team, chunk, width), f32),
        ((team, chunk, width), f32),
        ((team, chunk, width), f32),
        ((blks, team, chunk, width), f32),
    ]
    results = pl.pallas_call(
        functools.partial(kernel, blks, team),
        out_shape=outs,
        in_specs=[vmem, vmem, vmem, vmem, pl.BlockSpec(memory_space=pltpu.SMEM), anywhere],
        out_specs=(vmem,) * 4,
        scratch_shapes=[pltpu.VMEM(shape, kind) for shape, kind in buffers]
        + [dma]
        + [dma((team,))] * 8
        + [dma((blks,))] * 6
        + [dma((team,))] * 4
        + [dma((blks,))] * 2,
        compiler_params=pltpu.CompilerParams(
            collective_id=0, has_side_effects=True, vmem_limit_bytes=56 * 2**20
        ),
    )(features, weight, bias.reshape(1, width), cotangent, adj_cols, adj_vals)
    hidden, grad_input, grad_weight, grad_bias = pl.pallas_call(
        hand_out,
        out_shape=outs,
        in_specs=[anywhere] * 4,
        out_specs=(anywhere,) * 4,
        scratch_shapes=[pltpu.VMEM(out.shape, out.dtype) for out in outs]
        + [dma((4,)), dma((4,))],
        compiler_params=pltpu.CompilerParams(vmem_limit_bytes=56 * 2**20),
    )(*results)
    return hidden, grad_input, grad_weight, grad_bias.reshape(width)


def solution(mesh):
    return jax.shard_map(
        functools.partial(local, mesh.shape["blk"], mesh.shape["team"]),
        mesh=mesh,
        in_specs=(
            P(("blk", "team"), None),
            P(),
            P(),
            P(("blk", "team"), None),
            P("team", None, "blk", None),
            P("team", None, "blk", None, None, None),
        ),
        out_specs=(P(("blk", "team"), None), P(("blk", "team"), None), P(), P()),
        check_vma=False,
    )
```

```python
import functools

import jax
import jax.numpy as jnp
from jax import lax
from jax.experimental import pallas as pl
from jax.experimental.pallas import tpu as pltpu
from jax.sharding import PartitionSpec as P

PLANE = 4
MESH = pl.DeviceIdType.MESH


def flip(index, mask):
    bit = 1
    while bit <= mask:
        if mask & bit:
            index = index + bit - 2 * bit * ((index // bit) % 2)
        bit *= 2
    return index


def kernel(
    blks,
    team,
    x_ref,
    w_ref,
    b_ref,
    ct_ref,
    cols_ref,
    vals_ref,
    hidden_ref,
    gi_ref,
    gw_ref,
    gb_ref,
    w_own,
    b_own,
    ct_own,
    cols,
    vals,
    dense,
    xbuf,
    pbuf,
    part,
    back,
    ybuf,
    sbuf,
    gpart,
    gl1,
    gtot,
    grs,
    gag,
    sums,
    in_sem,
    x_send,
    x_recv,
    x_send2,
    x_recv2,
    p_send,
    p_recv,
    p_send2,
    p_recv2,
    y_send,
    y_recv,
    s_send,
    s_recv,
    l1_send,
    l1_recv,
    rs_send,
    rs_recv,
    ag_send,
    ag_recv,
    l4_send,
    l4_recv,
):
    g = lax.axis_index("blk")
    m = lax.axis_index("team")
    block = x_ref.shape[0]
    width = x_ref.shape[1]
    nnz = vals_ref.shape[3]
    half = block // 2
    line = team // PLANE
    fars = list(range(PLANE, team, PLANE))

    barrier = pltpu.get_barrier_semaphore()
    partners = list(range(1, PLANE)) + fars
    for mask in partners:
        pl.semaphore_signal(
            barrier, inc=1, device_id=(g, flip(m, mask)), device_id_type=MESH
        )
    for mask in range(1, blks):
        pl.semaphore_signal(
            barrier, inc=1, device_id=(flip(g, mask), m), device_id_type=MESH
        )

    def place(mask):
        return (mask % PLANE) * line + mask // PLANE

    def rows_of(mask, start=0, size=block):
        first = place(mask) * block + start
        return pl.ds(first, size)

    fetches = [
        pltpu.make_async_copy(src, dst, in_sem.at[i])
        for i, (src, dst) in enumerate(
            (
                (x_ref, xbuf.at[rows_of(0)]),
                (cols_ref, cols),
                (vals_ref, vals),
                (w_ref, w_own),
                (b_ref, b_own),
                (ct_ref, ct_own),
            )
        )
    ]
    for fetch in fetches:
        fetch.start()

    def lay(i, carry):
        mask = (i % line) * PLANE + i // line
        c = 0
        bit = 1
        while bit < team:
            c = c + bit * ((m // bit + mask // bit) % 2)
            bit *= 2
        for r in range(blks):
            slot = 0
            found = 0
            for k in range(nnz):
                hit = cols[0, r, 0, k] == c
                slot = jnp.where(hit, k, slot)
                found = jnp.where(hit, 1, found)
            keep = found.astype(jnp.float32)
            item = vals[0, r, 0, slot].astype(jnp.float32) * keep
            span = pl.ds(pl.multiple_of(i * block, block), block)
            dense[r * block : (r + 1) * block, span] = item.astype(jnp.bfloat16)
        return carry

    fetches[0].wait()
    pl.semaphore_wait(barrier, len(partners) + blks - 1)

    pending = []

    def send(src, dst, send_sem, recv_sem, device):
        copy = pltpu.make_async_remote_copy(
            src_ref=src,
            dst_ref=dst,
            send_sem=send_sem,
            recv_sem=recv_sem,
            device_id=device,
            device_id_type=MESH,
        )
        copy.start()
        pending.append(copy)

    def arrived(dst, send_sem, recv_sem):
        pltpu.make_async_remote_copy(
            src_ref=dst,
            dst_ref=dst,
            send_sem=send_sem,
            recv_sem=recv_sem,
            device_id=(g, flip(m, 1)),
            device_id_type=MESH,
        ).wait_recv()

    class Gather:
        def __init__(self, buf, sends, recvs, sends2, recvs2):
            self.buf = buf
            self.sems = (sends, recvs)
            self.sems2 = (sends2, recvs2)

        def item(self, mask):
            return self.buf.at[rows_of(mask)]

        def spread(self, far):
            for near in (1, 2):
                mask = far + near
                sends, recvs = self.sems
                send(
                    self.item(far),
                    self.item(mask),
                    sends.at[mask],
                    recvs.at[mask],
                    (g, flip(m, near)),
                )

        def open(self):
            sends, recvs = self.sems
            for far in fars:
                send(
                    self.item(0),
                    self.item(far),
                    sends.at[far],
                    recvs.at[far],
                    (g, flip(m, far)),
                )
            self.spread(0)

        def wait(self, mask):
            sends, recvs = self.sems
            arrived(self.item(mask), sends.at[mask], recvs.at[mask])

        def forward(self, far):
            self.wait(far)
            self.spread(far)

        def cross(self, far):
            mask = far + 3
            for near, sems, start in ((1, self.sems, 0), (2, self.sems2, half)):
                self.wait(far + near)
                send(
                    self.buf.at[rows_of(far + near, start, half)],
                    self.buf.at[rows_of(mask, start, half)],
                    sems[0].at[mask],
                    sems[1].at[mask],
                    (g, flip(m, 3 - near)),
                )

        def close(self):
            for far in [0] + fars:
                mask = far + 3
                for sems, start in ((self.sems, 0), (self.sems2, half)):
                    item = self.buf.at[rows_of(mask, start, half)]
                    arrived(item, sems[0].at[mask], sems[1].at[mask])

    def exchange(src_of, buf, send_sems, recv_sems):
        for mask in range(1, blks):
            peer = flip(g, mask)
            send(src_of(peer), buf.at[g], send_sems.at[mask], recv_sems.at[mask], (peer, m))

    def exchanged(buf, send_sems, recv_sems):
        for mask in range(1, blks):
            arrived(buf.at[flip(g, mask)], send_sems.at[mask], recv_sems.at[mask])

    deep = line * block
    tall = min(2, blks) * block

    def gain(buf, near, out):
        span = slice(near * deep, (near + 1) * deep)
        for top in range(0, blks * block, tall):
            term = jnp.dot(
                dense[top : top + tall, span],
                buf[span, :],
                preferred_element_type=jnp.float32,
            ).reshape(tall // block, block, width)
            groups = pl.ds(top // block, tall // block)
            if near == 0:
                out[groups, :block] = term
            else:
                out[groups, :block] += term

    def tally(near):
        for far in [0] + fars:
            mask = near + far
            sums[flip(m, mask)] = jnp.sum(
                pbuf[rows_of(mask), :].astype(jnp.float32).reshape(block // 8, 8, width),
                axis=0,
            )

    xs = Gather(xbuf, x_send, x_recv, x_send2, x_recv2)
    xs.open()
    for fetch in fetches[1:]:
        fetch.wait()
    lax.fori_loop(0, line, lay, 0)
    for far in fars:
        xs.forward(far)
        xs.cross(far - PLANE)
    lax.fori_loop(line, 2 * line, lay, 0)
    gain(xbuf, 0, part)
    xs.cross(fars[-1])
    lax.fori_loop(2 * line, 4 * line, lay, 0)
    gain(xbuf, 1, part)
    gain(xbuf, 2, part)
    xs.close()
    gain(xbuf, 3, part)
    exchange(lambda peer: part.at[peer], ybuf, y_send, y_recv)
    y = part[g]
    exchanged(ybuf, y_send, y_recv)
    for mask in range(1, blks):
        y = y + ybuf[flip(g, mask)]
    high = y.astype(jnp.bfloat16)
    low = (y - high.astype(jnp.float32)).astype(jnp.bfloat16)
    weight = w_own[...]
    pre = (
        jnp.dot(high, weight, preferred_element_type=jnp.float32)
        + jnp.dot(low, weight, preferred_element_type=jnp.float32)
        + b_own[...]
    )
    square = pre * pre
    bent = jnp.tanh(0.7978845608 * (pre + 0.044715 * (square * pre)))
    gate = 0.5 * (1.0 + bent)
    slope = gate + (0.5 * pre) * ((1.0 - bent) * (1.0 + bent)) * (
        0.7978845608 * (1.0 + 0.134145 * square)
    )
    pulled = (ct_own[...].astype(jnp.float32) * slope).astype(jnp.bfloat16)

    pbuf[rows_of(0), :] = pulled
    forward_sends = pending[:]
    del pending[:]
    ps = Gather(pbuf, p_send, p_recv, p_send2, p_recv2)
    ps.open()
    turned = (((0,), (0,)), ((), ()))
    grad = lax.dot_general(high, pulled, turned, preferred_element_type=jnp.float32)
    grad = grad + lax.dot_general(low, pulled, turned, preferred_element_type=jnp.float32)
    chunk = gpart.shape[2]
    count = width // chunk
    chunks = blks * team
    whole = grad.reshape(count, chunk, width)
    if count < chunks:
        empty = jnp.zeros((chunks - count, chunk, width), jnp.float32)
        whole = jnp.concatenate([whole, empty], axis=0)
    gpart[...] = whole.reshape(blks, team, chunk, width)
    exchange(lambda peer: gpart.at[peer], gl1, l1_send, l1_recv)
    ps.forward(fars[0])

    exchanged(gl1, l1_send, l1_recv)
    total = gpart[g]
    for mask in range(1, blks):
        total = total + gl1[flip(g, mask)]
    gtot[...] = total
    for mask in range(1, team):
        peer = flip(m, mask)
        send(gtot.at[peer], grs.at[m], rs_send.at[mask], rs_recv.at[mask], (g, peer))
    grs[m] = gtot[m]
    hidden_ref[...] = (pre * gate).astype(jnp.bfloat16)

    ps.cross(0)
    for far in fars[1:]:
        ps.forward(far)
        ps.cross(far - PLANE)
    for mask in range(1, team):
        arrived(grs.at[flip(m, mask)], rs_send.at[mask], rs_recv.at[mask])
    gag[g, m] = jnp.sum(grs[...], axis=0)
    for mask in range(1, team):
        item = gag.at[g, m]
        send(item, item, ag_send.at[mask], ag_recv.at[mask], (g, flip(m, mask)))
    for copy in forward_sends:
        copy.wait_send()
    gain(pbuf, 0, back)
    tally(0)
    ps.cross(fars[-1])
    gain(pbuf, 1, back)
    gain(pbuf, 2, back)
    tally(1)
    tally(2)
    ps.close()
    gain(pbuf, 3, back)
    tally(3)
    for r in range(blks):
        back[r, block:] = jnp.sum(sums[...], axis=0)
    earlier = pending[:]
    del pending[:]
    exchange(lambda peer: back.at[peer], sbuf, s_send, s_recv)
    for mask in range(1, team):
        arrived(gag.at[g, flip(m, mask)], ag_send.at[mask], ag_recv.at[mask])
    exchange(lambda peer: gag.at[g], gag, l4_send, l4_recv)
    for copy in earlier:
        copy.wait_send()
    spread = back[g]
    exchanged(sbuf, s_send, s_recv)
    for mask in range(1, blks):
        spread = spread + sbuf[flip(g, mask)]
    gi_ref[...] = lax.dot_general(
        spread[:block].astype(jnp.bfloat16),
        weight,
        (((1,), (1,)), ((), ())),
        preferred_element_type=jnp.float32,
    ).astype(jnp.bfloat16)
    gb_ref[...] = jnp.sum(spread[block:], axis=0, keepdims=True)
    exchanged(gag, l4_send, l4_recv)
    gw_ref[...] = gag[...].reshape(chunks * chunk, width)[:width]
    for copy in pending:
        copy.wait_send()


def hand_out(*refs):
    count = len(refs) // 3
    takes, gives, slots, (into, out) = (
        refs[:count],
        refs[count : 2 * count],
        refs[2 * count : 3 * count],
        refs[3 * count :],
    )
    first = [pltpu.make_async_copy(takes[i], slots[i], into.at[i]) for i in range(count)]
    second = [pltpu.make_async_copy(slots[i], gives[i], out.at[i]) for i in range(count)]
    for copy in first:
        copy.start()
    for copy, onward in zip(first, second):
        copy.wait()
        onward.start()
    for copy in second:
        copy.wait()


def local(blks, team, features, weight, bias, cotangent, adj_cols, adj_vals):
    block, width = features.shape
    chunk = 8 * pl.cdiv(width, 8 * blks * team)
    f32, bf16 = jnp.float32, jnp.bfloat16
    dma = pltpu.SemaphoreType.DMA
    vmem = pl.BlockSpec(memory_space=pltpu.VMEM)
    anywhere = pl.BlockSpec(memory_space=pl.ANY)
    panels = blks * block
    outs = (
        jax.ShapeDtypeStruct((block, width), bf16),
        jax.ShapeDtypeStruct((block, width), bf16),
        jax.ShapeDtypeStruct((width, width), f32),
        jax.ShapeDtypeStruct((1, width), f32),
    )
    buffers = [
        ((width, width), bf16),
        ((1, width), f32),
        ((block, width), bf16),
        (adj_vals.shape, bf16),
        ((panels, team * block), bf16),
        ((team * block, width), bf16),
        ((team * block, width), bf16),
        ((blks, block, width), f32),
        ((blks, block + 8, width), f32),
        ((blks, block, width), f32),
        ((blks, block + 8, width), f32),
        ((blks, team, chunk, width), f32),
        ((blks, team, chunk, width), f32),
        ((team, chunk, width), f32),
        ((team, chunk, width), f32),
        ((blks, team, chunk, width), f32),
        ((team, 8, width), f32),
    ]
    results = pl.pallas_call(
        functools.partial(kernel, blks, team),
        out_shape=outs,
        in_specs=[anywhere] * 6,
        out_specs=(vmem,) * 4,
        scratch_shapes=[pltpu.VMEM(shape, kind) for shape, kind in buffers[:3]]
        + [pltpu.SMEM(adj_cols.shape, jnp.int32)]
        + [pltpu.VMEM(shape, kind) for shape, kind in buffers[3:]]
        + [dma((6,))]
        + [dma((team,))] * 8
        + [dma((blks,))] * 6
        + [dma((team,))] * 4
        + [dma((blks,))] * 2,
        compiler_params=pltpu.CompilerParams(
            collective_id=0, has_side_effects=True, vmem_limit_bytes=56 * 2**20
        ),
    )(features, weight, bias.reshape(1, width), cotangent, adj_cols, adj_vals)
    hidden, grad_input, grad_weight, grad_bias = pl.pallas_call(
        hand_out,
        out_shape=outs,
        in_specs=[anywhere] * 4,
        out_specs=(anywhere,) * 4,
        scratch_shapes=[pltpu.VMEM(out.shape, out.dtype) for out in outs]
        + [dma((4,)), dma((4,))],
        compiler_params=pltpu.CompilerParams(vmem_limit_bytes=56 * 2**20),
    )(*results)
    return hidden, grad_input, grad_weight, grad_bias.reshape(width)


def solution(mesh):
    return jax.shard_map(
        functools.partial(local, mesh.shape["blk"], mesh.shape["team"]),
        mesh=mesh,
        in_specs=(
            P(("blk", "team"), None),
            P(),
            P(),
            P(("blk", "team"), None),
            P("team", None, "blk", None),
            P("team", None, "blk", None, None, None),
        ),
        out_specs=(P(("blk", "team"), None), P(("blk", "team"), None), P(), P()),
        check_vma=False,
    )
```

```python
import functools

import jax
import jax.numpy as jnp
from jax import lax
from jax.experimental import pallas as pl
from jax.experimental.pallas import tpu as pltpu
from jax.sharding import PartitionSpec as P

PLANE = 4
MESH = pl.DeviceIdType.MESH


def flip(index, mask):
    bit = 1
    while bit <= mask:
        if mask & bit:
            index = index + bit - 2 * bit * ((index // bit) % 2)
        bit *= 2
    return index


def kernel(
    blks,
    team,
    x_ref,
    w_ref,
    b_ref,
    ct_ref,
    cols_ref,
    vals_ref,
    hidden_ref,
    gi_ref,
    gw_ref,
    gb_ref,
    w_own,
    b_own,
    ct_own,
    cols,
    vals,
    dense,
    xbuf,
    pbuf,
    part,
    back,
    ybuf,
    sbuf,
    gpart,
    gl1,
    gtot,
    grs,
    gag,
    sums,
    in_sem,
    x_send,
    x_recv,
    x_send2,
    x_recv2,
    p_send,
    p_recv,
    p_send2,
    p_recv2,
    y_send,
    y_recv,
    s_send,
    s_recv,
    l1_send,
    l1_recv,
    rs_send,
    rs_recv,
    ag_send,
    ag_recv,
    l4_send,
    l4_recv,
):
    g = lax.axis_index("blk")
    m = lax.axis_index("team")
    block = x_ref.shape[0]
    width = x_ref.shape[1]
    nnz = vals_ref.shape[3]
    half = block // 2
    line = team // PLANE
    z = m // PLANE
    last = line - 1

    barrier = pltpu.get_barrier_semaphore()

    def greet(device):
        pl.semaphore_signal(barrier, inc=1, device_id=device, device_id_type=MESH)

    pl.when(z < last)(lambda: greet((g, m + PLANE)))
    pl.when(z > 0)(lambda: greet((g, m - PLANE)))
    for near in (1, 2):
        greet((g, flip(m, near)))
    for mask in range(1, blks):
        greet((flip(g, mask), m))

    def rows_of(near, k, start=0, size=block):
        first = (near * line + k) * block + start
        if not isinstance(first, int):
            first = pl.multiple_of(first, half)
        return pl.ds(first, size)

    def owner(near, k):
        return flip((z + k) % line * PLANE + m % PLANE, near)

    def nth(n):
        both = jnp.minimum(z, last - z)
        paired = n <= 2 * both
        distance = jnp.where(paired, (n + 1) // 2, n - both)
        above = jnp.where(paired, n % 2 == 1, z < last - z)
        return jnp.where(above, distance, line - distance)

    order = [0] + [nth(n) for n in range(1, line)]

    fetches = [
        pltpu.make_async_copy(src, dst, in_sem.at[i])
        for i, (src, dst) in enumerate(
            (
                (x_ref, xbuf.at[rows_of(0, 0)]),
                (cols_ref, cols),
                (vals_ref, vals),
                (w_ref, w_own),
                (b_ref, b_own),
                (ct_ref, ct_own),
            )
        )
    ]
    for fetch in fetches:
        fetch.start()

    def lay(i, carry):
        near = i // line
        near1, near2 = near % 2, near // 2
        p1, p2 = m % 2, m // 2 % 2
        c = (z + i) % line * PLANE + (p2 + near2) % 2 * 2 + (p1 + near1) % 2
        for r in range(blks):
            slot = 0
            found = 0
            for k in range(nnz):
                hit = cols[0, r, 0, k] == c
                slot = jnp.where(hit, k, slot)
                found = jnp.where(hit, 1, found)
            keep = found.astype(jnp.float32)
            item = vals[0, r, 0, slot].astype(jnp.float32) * keep
            span = pl.ds(pl.multiple_of(i * block, block), block)
            dense[r * block : (r + 1) * block, span] = item.astype(jnp.bfloat16)
        return carry

    fetches[0].wait()
    pl.semaphore_wait(
        barrier, 1 + blks + (z < last).astype(jnp.int32) + (z > 0).astype(jnp.int32)
    )

    pending = []

    def send(src, dst, send_sem, recv_sem, device, when=None):
        copy = pltpu.make_async_remote_copy(
            src_ref=src,
            dst_ref=dst,
            send_sem=send_sem,
            recv_sem=recv_sem,
            device_id=device,
            device_id_type=MESH,
        )
        if when is None:
            copy.start()
        else:
            pl.when(when)(copy.start)
        pending.append((copy, when))

    def sent(copies):
        for copy, when in copies:
            if when is None:
                copy.wait_send()
            else:
                pl.when(when)(copy.wait_send)

    def arrived(dst, send_sem, recv_sem):
        pltpu.make_async_remote_copy(
            src_ref=dst,
            dst_ref=dst,
            send_sem=send_sem,
            recv_sem=recv_sem,
            device_id=(g, flip(m, 1)),
            device_id_type=MESH,
        ).wait_recv()

    class Gather:
        def __init__(self, buf, sends, recvs, sends2, recvs2):
            self.buf = buf
            self.sems = (sends, recvs)
            self.sems2 = (sends2, recvs2)

        def item(self, near, k):
            return self.buf.at[rows_of(near, k)]

        def move(self, k, to, device, when, send_sem):
            recvs = self.sems[1]
            send(self.item(0, k), self.item(0, to), send_sem, recvs.at[to], device, when)

        def spread(self, k):
            sends, recvs = self.sems
            for near in (1, 2):
                at = near * line + k
                send(
                    self.item(0, k),
                    self.item(near, k),
                    sends.at[at],
                    recvs.at[at],
                    (g, flip(m, near)),
                )

        def open(self):
            sends, sends2 = self.sems[0], self.sems2[0]
            self.move(0, last, (g, m + PLANE), z < last, sends.at[0])
            self.move(0, 1 % line, (g, m - PLANE), z > 0, sends2.at[0])
            self.spread(0)

        def wait(self, near, k):
            sends, recvs = self.sems
            at = near * line + k
            arrived(self.item(near, k), sends.at[at], recvs.at[at])

        def forward(self, n):
            k = order[n]
            sends, sends2 = self.sems[0], self.sems2[0]
            self.wait(0, k)
            down = jnp.logical_and(z + k < line, z > 0)
            up = jnp.logical_and(z + k >= line, z < last)
            self.move(k, (k + 1) % line, (g, m - PLANE), down, sends.at[k])
            self.move(k, (k - 1) % line, (g, m + PLANE), up, sends2.at[k])
            self.spread(k)

        def cross(self, n):
            k = order[n]
            at = 3 * line + k
            for near, sems, start in ((1, self.sems, 0), (2, self.sems2, half)):
                self.wait(near, k)
                send(
                    self.buf.at[rows_of(near, k, start, half)],
                    self.buf.at[rows_of(3, k, start, half)],
                    sems[0].at[at],
                    sems[1].at[at],
                    (g, flip(m, 3 - near)),
                )

        def close(self):
            for k in range(line):
                at = 3 * line + k
                for sems, start in ((self.sems, 0), (self.sems2, half)):
                    item = self.buf.at[rows_of(3, k, start, half)]
                    arrived(item, sems[0].at[at], sems[1].at[at])

    def exchange(src_of, buf, send_sems, recv_sems):
        for mask in range(1, blks):
            peer = flip(g, mask)
            send(src_of(peer), buf.at[g], send_sems.at[mask], recv_sems.at[mask], (peer, m))

    def exchanged(buf, send_sems, recv_sems):
        for mask in range(1, blks):
            arrived(buf.at[flip(g, mask)], send_sems.at[mask], recv_sems.at[mask])

    deep = line * block
    tall = min(2, blks) * block

    def gain(buf, near, out):
        span = slice(near * deep, (near + 1) * deep)
        for top in range(0, blks * block, tall):
            term = jnp.dot(
                dense[top : top + tall, span],
                buf[span, :],
                preferred_element_type=jnp.float32,
            ).reshape(tall // block, block, width)
            groups = pl.ds(top // block, tall // block)
            if near == 0:
                out[groups, :block] = term
            else:
                out[groups, :block] += term

    def tally(near):
        for k in range(line):
            sums[owner(near, k)] = jnp.sum(
                pbuf[rows_of(near, k), :].astype(jnp.float32).reshape(block // 8, 8, width),
                axis=0,
            )

    xs = Gather(xbuf, x_send, x_recv, x_send2, x_recv2)
    xs.open()
    for fetch in fetches[1:]:
        fetch.wait()
    lax.fori_loop(0, line, lay, 0)
    for n in range(1, line):
        xs.forward(n)
        xs.cross(n - 1)
    lax.fori_loop(line, 2 * line, lay, 0)
    gain(xbuf, 0, part)
    xs.cross(last)
    lax.fori_loop(2 * line, 4 * line, lay, 0)
    gain(xbuf, 1, part)
    gain(xbuf, 2, part)
    xs.close()
    gain(xbuf, 3, part)
    exchange(lambda peer: part.at[peer], ybuf, y_send, y_recv)
    y = part[g]
    exchanged(ybuf, y_send, y_recv)
    for mask in range(1, blks):
        y = y + ybuf[flip(g, mask)]
    high = y.astype(jnp.bfloat16)
    low = (y - high.astype(jnp.float32)).astype(jnp.bfloat16)
    weight = w_own[...]
    pre = (
        jnp.dot(high, weight, preferred_element_type=jnp.float32)
        + jnp.dot(low, weight, preferred_element_type=jnp.float32)
        + b_own[...]
    )
    square = pre * pre
    bent = jnp.tanh(0.7978845608 * (pre + 0.044715 * (square * pre)))
    gate = 0.5 * (1.0 + bent)
    slope = gate + (0.5 * pre) * ((1.0 - bent) * (1.0 + bent)) * (
        0.7978845608 * (1.0 + 0.134145 * square)
    )
    pulled = (ct_own[...].astype(jnp.float32) * slope).astype(jnp.bfloat16)

    pbuf[rows_of(0, 0), :] = pulled
    forward_sends = pending[:]
    del pending[:]
    ps = Gather(pbuf, p_send, p_recv, p_send2, p_recv2)
    ps.open()
    turned = (((0,), (0,)), ((), ()))
    grad = lax.dot_general(high, pulled, turned, preferred_element_type=jnp.float32)
    grad = grad + lax.dot_general(low, pulled, turned, preferred_element_type=jnp.float32)
    chunk = gpart.shape[2]
    count = width // chunk
    chunks = blks * team
    whole = grad.reshape(count, chunk, width)
    if count < chunks:
        empty = jnp.zeros((chunks - count, chunk, width), jnp.float32)
        whole = jnp.concatenate([whole, empty], axis=0)
    gpart[...] = whole.reshape(blks, team, chunk, width)
    exchange(lambda peer: gpart.at[peer], gl1, l1_send, l1_recv)
    ps.forward(1)

    exchanged(gl1, l1_send, l1_recv)
    total = gpart[g]
    for mask in range(1, blks):
        total = total + gl1[flip(g, mask)]
    gtot[...] = total
    for mask in range(1, team):
        peer = flip(m, mask)
        send(gtot.at[peer], grs.at[m], rs_send.at[mask], rs_recv.at[mask], (g, peer))
    grs[m] = gtot[m]
    hidden_ref[...] = (pre * gate).astype(jnp.bfloat16)

    ps.cross(0)
    for n in range(2, line):
        ps.forward(n)
        ps.cross(n - 1)
    for mask in range(1, team):
        arrived(grs.at[flip(m, mask)], rs_send.at[mask], rs_recv.at[mask])
    gag[g, m] = jnp.sum(grs[...], axis=0)
    for mask in range(1, team):
        item = gag.at[g, m]
        send(item, item, ag_send.at[mask], ag_recv.at[mask], (g, flip(m, mask)))
    sent(forward_sends)
    gain(pbuf, 0, back)
    tally(0)
    ps.cross(last)
    gain(pbuf, 1, back)
    gain(pbuf, 2, back)
    tally(1)
    tally(2)
    ps.close()
    gain(pbuf, 3, back)
    tally(3)
    for r in range(blks):
        back[r, block:] = jnp.sum(sums[...], axis=0)
    earlier = pending[:]
    del pending[:]
    exchange(lambda peer: back.at[peer], sbuf, s_send, s_recv)
    for mask in range(1, team):
        arrived(gag.at[g, flip(m, mask)], ag_send.at[mask], ag_recv.at[mask])
    exchange(lambda peer: gag.at[g], gag, l4_send, l4_recv)
    sent(earlier)
    spread = back[g]
    exchanged(sbuf, s_send, s_recv)
    for mask in range(1, blks):
        spread = spread + sbuf[flip(g, mask)]
    gi_ref[...] = lax.dot_general(
        spread[:block].astype(jnp.bfloat16),
        weight,
        (((1,), (1,)), ((), ())),
        preferred_element_type=jnp.float32,
    ).astype(jnp.bfloat16)
    gb_ref[...] = jnp.sum(spread[block:], axis=0, keepdims=True)
    exchanged(gag, l4_send, l4_recv)
    gw_ref[...] = gag[...].reshape(chunks * chunk, width)[:width]
    sent(pending)


def hand_out(*refs):
    count = len(refs) // 3
    takes, gives, slots, (into, out) = (
        refs[:count],
        refs[count : 2 * count],
        refs[2 * count : 3 * count],
        refs[3 * count :],
    )
    first = [pltpu.make_async_copy(takes[i], slots[i], into.at[i]) for i in range(count)]
    second = [pltpu.make_async_copy(slots[i], gives[i], out.at[i]) for i in range(count)]
    for copy in first:
        copy.start()
    for copy, onward in zip(first, second):
        copy.wait()
        onward.start()
    for copy in second:
        copy.wait()


def local(blks, team, features, weight, bias, cotangent, adj_cols, adj_vals):
    block, width = features.shape
    chunk = 8 * pl.cdiv(width, 8 * blks * team)
    f32, bf16 = jnp.float32, jnp.bfloat16
    dma = pltpu.SemaphoreType.DMA
    vmem = pl.BlockSpec(memory_space=pltpu.VMEM)
    anywhere = pl.BlockSpec(memory_space=pl.ANY)
    panels = blks * block
    outs = (
        jax.ShapeDtypeStruct((block, width), bf16),
        jax.ShapeDtypeStruct((block, width), bf16),
        jax.ShapeDtypeStruct((width, width), f32),
        jax.ShapeDtypeStruct((1, width), f32),
    )
    buffers = [
        ((width, width), bf16),
        ((1, width), f32),
        ((block, width), bf16),
        (adj_vals.shape, bf16),
        ((panels, team * block), bf16),
        ((team * block, width), bf16),
        ((team * block, width), bf16),
        ((blks, block, width), f32),
        ((blks, block + 8, width), f32),
        ((blks, block, width), f32),
        ((blks, block + 8, width), f32),
        ((blks, team, chunk, width), f32),
        ((blks, team, chunk, width), f32),
        ((team, chunk, width), f32),
        ((team, chunk, width), f32),
        ((blks, team, chunk, width), f32),
        ((team, 8, width), f32),
    ]
    results = pl.pallas_call(
        functools.partial(kernel, blks, team),
        out_shape=outs,
        in_specs=[anywhere] * 6,
        out_specs=(vmem,) * 4,
        scratch_shapes=[pltpu.VMEM(shape, kind) for shape, kind in buffers[:3]]
        + [pltpu.SMEM(adj_cols.shape, jnp.int32)]
        + [pltpu.VMEM(shape, kind) for shape, kind in buffers[3:]]
        + [dma((6,))]
        + [dma((team,))] * 8
        + [dma((blks,))] * 6
        + [dma((team,))] * 4
        + [dma((blks,))] * 2,
        compiler_params=pltpu.CompilerParams(
            collective_id=0, has_side_effects=True, vmem_limit_bytes=56 * 2**20
        ),
    )(features, weight, bias.reshape(1, width), cotangent, adj_cols, adj_vals)
    hidden, grad_input, grad_weight, grad_bias = pl.pallas_call(
        hand_out,
        out_shape=outs,
        in_specs=[anywhere] * 4,
        out_specs=(anywhere,) * 4,
        scratch_shapes=[pltpu.VMEM(out.shape, out.dtype) for out in outs]
        + [dma((4,)), dma((4,))],
        compiler_params=pltpu.CompilerParams(vmem_limit_bytes=56 * 2**20),
    )(*results)
    return hidden, grad_input, grad_weight, grad_bias.reshape(width)


def solution(mesh):
    return jax.shard_map(
        functools.partial(local, mesh.shape["blk"], mesh.shape["team"]),
        mesh=mesh,
        in_specs=(
            P(("blk", "team"), None),
            P(),
            P(),
            P(("blk", "team"), None),
            P("team", None, "blk", None),
            P("team", None, "blk", None, None, None),
        ),
        out_specs=(P(("blk", "team"), None), P(("blk", "team"), None), P(), P()),
        check_vma=False,
    )
```

```python
import functools

import jax
import jax.numpy as jnp
from jax import lax
from jax.experimental import pallas as pl
from jax.experimental.pallas import tpu as pltpu
from jax.sharding import PartitionSpec as P

PLANE = 4
MESH = pl.DeviceIdType.MESH


def flip(index, mask):
    bit = 1
    while bit <= mask:
        if mask & bit:
            index = index + bit - 2 * bit * ((index // bit) % 2)
        bit *= 2
    return index


def kernel(
    blks,
    team,
    x_ref,
    w_ref,
    b_ref,
    ct_ref,
    cols_ref,
    vals_ref,
    hidden_ref,
    gi_ref,
    gw_ref,
    gb_ref,
    w_own,
    b_own,
    ct_own,
    cols,
    vals,
    dense,
    xbuf,
    pbuf,
    part,
    back,
    ybuf,
    sbuf,
    gpart,
    gl1,
    gtot,
    grs,
    gag,
    sums,
    in_sem,
    x_send,
    x_recv,
    p_send,
    p_recv,
    y_send,
    y_recv,
    s_send,
    s_recv,
    l1_send,
    l1_recv,
    rs_send,
    rs_recv,
    ag_send,
    ag_recv,
    l4_send,
    l4_recv,
):
    g = lax.axis_index("blk")
    m = lax.axis_index("team")
    block = x_ref.shape[0]
    width = x_ref.shape[1]
    nnz = vals_ref.shape[3]
    line = team // PLANE
    fars = list(range(PLANE, team, PLANE))

    barrier = pltpu.get_barrier_semaphore()
    partners = list(range(1, PLANE)) + fars
    for mask in partners:
        pl.semaphore_signal(
            barrier, inc=1, device_id=(g, flip(m, mask)), device_id_type=MESH
        )
    for mask in range(1, blks):
        pl.semaphore_signal(
            barrier, inc=1, device_id=(flip(g, mask), m), device_id_type=MESH
        )

    def place(mask):
        return (mask % PLANE) * line + mask // PLANE

    def rows_of(mask):
        return pl.ds(place(mask) * block, block)

    fetches = [
        pltpu.make_async_copy(src, dst, in_sem.at[i])
        for i, (src, dst) in enumerate(
            (
                (x_ref, xbuf.at[rows_of(0)]),
                (cols_ref, cols),
                (vals_ref, vals),
                (w_ref, w_own),
                (b_ref, b_own),
                (ct_ref, ct_own),
            )
        )
    ]
    for fetch in fetches:
        fetch.start()

    def lay(i, carry):
        mask = (i % line) * PLANE + i // line
        c = 0
        bit = 1
        while bit < team:
            c = c + bit * ((m // bit + mask // bit) % 2)
            bit *= 2
        for r in range(blks):
            slot = 0
            found = 0
            for k in range(nnz):
                hit = cols[0, r, 0, k] == c
                slot = jnp.where(hit, k, slot)
                found = jnp.where(hit, 1, found)
            keep = found.astype(jnp.float32)
            item = vals[0, r, 0, slot].astype(jnp.float32) * keep
            span = pl.ds(pl.multiple_of(i * block, block), block)
            dense[r * block : (r + 1) * block, span] = item.astype(jnp.bfloat16)
        return carry

    fetches[0].wait()
    pl.semaphore_wait(barrier, len(partners) + blks - 1)

    pending = []

    def send(src, dst, send_sem, recv_sem, device):
        copy = pltpu.make_async_remote_copy(
            src_ref=src,
            dst_ref=dst,
            send_sem=send_sem,
            recv_sem=recv_sem,
            device_id=device,
            device_id_type=MESH,
        )
        copy.start()
        pending.append(copy)

    def arrived(dst, send_sem, recv_sem):
        pltpu.make_async_remote_copy(
            src_ref=dst,
            dst_ref=dst,
            send_sem=send_sem,
            recv_sem=recv_sem,
            device_id=(g, flip(m, 1)),
            device_id_type=MESH,
        ).wait_recv()

    class Gather:
        def __init__(self, buf, sends, recvs):
            self.buf = buf
            self.sems = (sends, recvs)

        def item(self, mask):
            return self.buf.at[rows_of(mask)]

        def spread(self, far):
            for near in (3, 1, 2):
                mask = far + near
                sends, recvs = self.sems
                send(
                    self.item(far),
                    self.item(mask),
                    sends.at[mask],
                    recvs.at[mask],
                    (g, flip(m, near)),
                )

        def open(self):
            sends, recvs = self.sems
            for far in fars:
                send(
                    self.item(0),
                    self.item(far),
                    sends.at[far],
                    recvs.at[far],
                    (g, flip(m, far)),
                )
            self.spread(0)

        def wait(self, mask):
            sends, recvs = self.sems
            arrived(self.item(mask), sends.at[mask], recvs.at[mask])

        def forward(self, far):
            self.wait(far)
            self.spread(far)

        def close(self, near):
            for far in [0] + fars:
                self.wait(far + near)

    def exchange(src_of, buf, send_sems, recv_sems):
        for mask in range(1, blks):
            peer = flip(g, mask)
            send(src_of(peer), buf.at[g], send_sems.at[mask], recv_sems.at[mask], (peer, m))

    def exchanged(buf, send_sems, recv_sems):
        for mask in range(1, blks):
            arrived(buf.at[flip(g, mask)], send_sems.at[mask], recv_sems.at[mask])

    deep = line * block
    tall = min(2, blks) * block

    def gain(buf, near, out):
        span = slice(near * deep, (near + 1) * deep)
        for top in range(0, blks * block, tall):
            term = jnp.dot(
                dense[top : top + tall, span],
                buf[span, :],
                preferred_element_type=jnp.float32,
            ).reshape(tall // block, block, width)
            groups = pl.ds(top // block, tall // block)
            if near == 0:
                out[groups, :block] = term
            else:
                out[groups, :block] += term

    def tally(near):
        for far in [0] + fars:
            mask = near + far
            sums[flip(m, mask)] = jnp.sum(
                pbuf[rows_of(mask), :].astype(jnp.float32).reshape(block // 8, 8, width),
                axis=0,
            )

    xs = Gather(xbuf, x_send, x_recv)
    xs.open()
    for fetch in fetches[1:]:
        fetch.wait()
    lax.fori_loop(0, line, lay, 0)
    for far in fars:
        xs.forward(far)
    lax.fori_loop(line, 4 * line, lay, 0)
    for near in range(PLANE):
        if near:
            xs.close(near)
        gain(xbuf, near, part)
    exchange(lambda peer: part.at[peer], ybuf, y_send, y_recv)
    y = part[g]
    exchanged(ybuf, y_send, y_recv)
    for mask in range(1, blks):
        y = y + ybuf[flip(g, mask)]
    high = y.astype(jnp.bfloat16)
    low = (y - high.astype(jnp.float32)).astype(jnp.bfloat16)
    weight = w_own[...]
    pre = (
        jnp.dot(high, weight, preferred_element_type=jnp.float32)
        + jnp.dot(low, weight, preferred_element_type=jnp.float32)
        + b_own[...]
    )
    square = pre * pre
    bent = jnp.tanh(0.7978845608 * (pre + 0.044715 * (square * pre)))
    gate = 0.5 * (1.0 + bent)
    slope = gate + (0.5 * pre) * ((1.0 - bent) * (1.0 + bent)) * (
        0.7978845608 * (1.0 + 0.134145 * square)
    )
    pulled = (ct_own[...].astype(jnp.float32) * slope).astype(jnp.bfloat16)

    pbuf[rows_of(0), :] = pulled
    forward_sends = pending[:]
    del pending[:]
    ps = Gather(pbuf, p_send, p_recv)
    ps.open()
    turned = (((0,), (0,)), ((), ()))
    grad = lax.dot_general(high, pulled, turned, preferred_element_type=jnp.float32)
    grad = grad + lax.dot_general(low, pulled, turned, preferred_element_type=jnp.float32)
    chunk = gpart.shape[2]
    count = width // chunk
    chunks = blks * team
    whole = grad.reshape(count, chunk, width)
    if count < chunks:
        empty = jnp.zeros((chunks - count, chunk, width), jnp.float32)
        whole = jnp.concatenate([whole, empty], axis=0)
    gpart[...] = whole.reshape(blks, team, chunk, width)
    exchange(lambda peer: gpart.at[peer], gl1, l1_send, l1_recv)
    ps.forward(fars[0])

    exchanged(gl1, l1_send, l1_recv)
    total = gpart[g]
    for mask in range(1, blks):
        total = total + gl1[flip(g, mask)]
    gtot[...] = total
    for mask in range(1, team):
        peer = flip(m, mask)
        send(gtot.at[peer], grs.at[m], rs_send.at[mask], rs_recv.at[mask], (g, peer))
    grs[m] = gtot[m]
    hidden_ref[...] = (pre * gate).astype(jnp.bfloat16)

    for far in fars[1:]:
        ps.forward(far)
    for mask in range(1, team):
        arrived(grs.at[flip(m, mask)], rs_send.at[mask], rs_recv.at[mask])
    gag[g, m] = jnp.sum(grs[...], axis=0)
    for mask in range(1, team):
        item = gag.at[g, m]
        send(item, item, ag_send.at[mask], ag_recv.at[mask], (g, flip(m, mask)))
    for copy in forward_sends:
        copy.wait_send()
    for near in range(PLANE):
        if near:
            ps.close(near)
        gain(pbuf, near, back)
        tally(near)
    for r in range(blks):
        back[r, block:] = jnp.sum(sums[...], axis=0)
    earlier = pending[:]
    del pending[:]
    exchange(lambda peer: back.at[peer], sbuf, s_send, s_recv)
    for mask in range(1, team):
        arrived(gag.at[g, flip(m, mask)], ag_send.at[mask], ag_recv.at[mask])
    exchange(lambda peer: gag.at[g], gag, l4_send, l4_recv)
    for copy in earlier:
        copy.wait_send()
    spread = back[g]
    exchanged(sbuf, s_send, s_recv)
    for mask in range(1, blks):
        spread = spread + sbuf[flip(g, mask)]
    gi_ref[...] = lax.dot_general(
        spread[:block].astype(jnp.bfloat16),
        weight,
        (((1,), (1,)), ((), ())),
        preferred_element_type=jnp.float32,
    ).astype(jnp.bfloat16)
    gb_ref[...] = jnp.sum(spread[block:], axis=0, keepdims=True)
    exchanged(gag, l4_send, l4_recv)
    gw_ref[...] = gag[...].reshape(chunks * chunk, width)[:width]
    for copy in pending:
        copy.wait_send()


def hand_out(*refs):
    count = len(refs) // 3
    takes, gives, slots, (into, out) = (
        refs[:count],
        refs[count : 2 * count],
        refs[2 * count : 3 * count],
        refs[3 * count :],
    )
    first = [pltpu.make_async_copy(takes[i], slots[i], into.at[i]) for i in range(count)]
    second = [pltpu.make_async_copy(slots[i], gives[i], out.at[i]) for i in range(count)]
    for copy in first:
        copy.start()
    for copy, onward in zip(first, second):
        copy.wait()
        onward.start()
    for copy in second:
        copy.wait()


def local(blks, team, features, weight, bias, cotangent, adj_cols, adj_vals):
    block, width = features.shape
    chunk = 8 * pl.cdiv(width, 8 * blks * team)
    f32, bf16 = jnp.float32, jnp.bfloat16
    dma = pltpu.SemaphoreType.DMA
    vmem = pl.BlockSpec(memory_space=pltpu.VMEM)
    anywhere = pl.BlockSpec(memory_space=pl.ANY)
    panels = blks * block
    outs = (
        jax.ShapeDtypeStruct((block, width), bf16),
        jax.ShapeDtypeStruct((block, width), bf16),
        jax.ShapeDtypeStruct((width, width), f32),
        jax.ShapeDtypeStruct((1, width), f32),
    )
    buffers = [
        ((width, width), bf16),
        ((1, width), f32),
        ((block, width), bf16),
        (adj_vals.shape, bf16),
        ((panels, team * block), bf16),
        ((team * block, width), bf16),
        ((team * block, width), bf16),
        ((blks, block, width), f32),
        ((blks, block + 8, width), f32),
        ((blks, block, width), f32),
        ((blks, block + 8, width), f32),
        ((blks, team, chunk, width), f32),
        ((blks, team, chunk, width), f32),
        ((team, chunk, width), f32),
        ((team, chunk, width), f32),
        ((blks, team, chunk, width), f32),
        ((team, 8, width), f32),
    ]
    results = pl.pallas_call(
        functools.partial(kernel, blks, team),
        out_shape=outs,
        in_specs=[anywhere] * 6,
        out_specs=(vmem,) * 4,
        scratch_shapes=[pltpu.VMEM(shape, kind) for shape, kind in buffers[:3]]
        + [pltpu.SMEM(adj_cols.shape, jnp.int32)]
        + [pltpu.VMEM(shape, kind) for shape, kind in buffers[3:]]
        + [dma((6,))]
        + [dma((team,))] * 4
        + [dma((blks,))] * 6
        + [dma((team,))] * 4
        + [dma((blks,))] * 2,
        compiler_params=pltpu.CompilerParams(
            collective_id=0, has_side_effects=True, vmem_limit_bytes=56 * 2**20
        ),
    )(features, weight, bias.reshape(1, width), cotangent, adj_cols, adj_vals)
    hidden, grad_input, grad_weight, grad_bias = pl.pallas_call(
        hand_out,
        out_shape=outs,
        in_specs=[anywhere] * 4,
        out_specs=(anywhere,) * 4,
        scratch_shapes=[pltpu.VMEM(out.shape, out.dtype) for out in outs]
        + [dma((4,)), dma((4,))],
        compiler_params=pltpu.CompilerParams(vmem_limit_bytes=56 * 2**20),
    )(*results)
    return hidden, grad_input, grad_weight, grad_bias.reshape(width)


def solution(mesh):
    return jax.shard_map(
        functools.partial(local, mesh.shape["blk"], mesh.shape["team"]),
        mesh=mesh,
        in_specs=(
            P(("blk", "team"), None),
            P(),
            P(),
            P(("blk", "team"), None),
            P("team", None, "blk", None),
            P("team", None, "blk", None, None, None),
        ),
        out_specs=(P(("blk", "team"), None), P(("blk", "team"), None), P(), P()),
        check_vma=False,
    )
```

```python
import functools

import jax
import jax.numpy as jnp
from jax import lax
from jax.experimental import pallas as pl
from jax.experimental.pallas import tpu as pltpu
from jax.sharding import PartitionSpec as P

PLANE = 4
MESH = pl.DeviceIdType.MESH


def flip(index, mask):
    bit = 1
    while bit <= mask:
        if mask & bit:
            index = index + bit - 2 * bit * ((index // bit) % 2)
        bit *= 2
    return index


def kernel(
    blks,
    team,
    x_ref,
    w_ref,
    b_ref,
    ct_ref,
    cols_ref,
    vals_ref,
    hidden_ref,
    gi_ref,
    gw_ref,
    gb_ref,
    w_own,
    b_own,
    ct_own,
    cols,
    vals,
    dense,
    xbuf,
    pbuf,
    part,
    back,
    ybuf,
    sbuf,
    gpart,
    gl1,
    gtot,
    grs,
    gag,
    sums,
    in_sem,
    x_send,
    x_recv,
    x_send2,
    x_recv2,
    p_send,
    p_recv,
    p_send2,
    p_recv2,
    y_send,
    y_recv,
    s_send,
    s_recv,
    l1_send,
    l1_recv,
    rs_send,
    rs_recv,
    ag_send,
    ag_recv,
    l4_send,
    l4_recv,
):
    g = lax.axis_index("blk")
    m = lax.axis_index("team")
    block = x_ref.shape[0]
    width = x_ref.shape[1]
    nnz = vals_ref.shape[3]
    half = block // 2
    line = team // PLANE
    fars = list(range(PLANE, team, PLANE))
    early = list(range(0, team // 2, PLANE))

    barrier = pltpu.get_barrier_semaphore()
    partners = list(range(1, PLANE)) + fars
    for mask in partners:
        pl.semaphore_signal(
            barrier, inc=1, device_id=(g, flip(m, mask)), device_id_type=MESH
        )
    for mask in range(1, blks):
        pl.semaphore_signal(
            barrier, inc=1, device_id=(flip(g, mask), m), device_id_type=MESH
        )

    def place(mask):
        return (mask % PLANE) * line + mask // PLANE

    def rows_of(mask, start=0, size=block):
        first = place(mask) * block + start
        return pl.ds(first, size)

    fetches = [
        pltpu.make_async_copy(src, dst, in_sem.at[i])
        for i, (src, dst) in enumerate(
            (
                (x_ref, xbuf.at[rows_of(0)]),
                (cols_ref, cols),
                (vals_ref, vals),
                (w_ref, w_own),
                (b_ref, b_own),
                (ct_ref, ct_own),
            )
        )
    ]
    for fetch in fetches:
        fetch.start()

    def lay(i, carry):
        mask = (i % line) * PLANE + i // line
        c = 0
        bit = 1
        while bit < team:
            c = c + bit * ((m // bit + mask // bit) % 2)
            bit *= 2
        for r in range(blks):
            slot = 0
            found = 0
            for k in range(nnz):
                hit = cols[0, r, 0, k] == c
                slot = jnp.where(hit, k, slot)
                found = jnp.where(hit, 1, found)
            keep = found.astype(jnp.float32)
            item = vals[0, r, 0, slot].astype(jnp.float32) * keep
            span = pl.ds(pl.multiple_of(i * block, block), block)
            dense[r * block : (r + 1) * block, span] = item.astype(jnp.bfloat16)
        return carry

    fetches[0].wait()
    pl.semaphore_wait(barrier, len(partners) + blks - 1)

    pending = []

    def send(src, dst, send_sem, recv_sem, device):
        copy = pltpu.make_async_remote_copy(
            src_ref=src,
            dst_ref=dst,
            send_sem=send_sem,
            recv_sem=recv_sem,
            device_id=device,
            device_id_type=MESH,
        )
        copy.start()
        pending.append(copy)

    def arrived(dst, send_sem, recv_sem):
        pltpu.make_async_remote_copy(
            src_ref=dst,
            dst_ref=dst,
            send_sem=send_sem,
            recv_sem=recv_sem,
            device_id=(g, flip(m, 1)),
            device_id_type=MESH,
        ).wait_recv()

    class Gather:
        def __init__(self, buf, sends, recvs, sends2, recvs2):
            self.buf = buf
            self.sems = (sends, recvs)
            self.sems2 = (sends2, recvs2)

        def item(self, mask):
            return self.buf.at[rows_of(mask)]

        def spread(self, far):
            for near in (1, 2) if far in early else (3, 1, 2):
                mask = far + near
                sends, recvs = self.sems
                send(
                    self.item(far),
                    self.item(mask),
                    sends.at[mask],
                    recvs.at[mask],
                    (g, flip(m, near)),
                )

        def open(self):
            sends, recvs = self.sems
            for far in fars:
                send(
                    self.item(0),
                    self.item(far),
                    sends.at[far],
                    recvs.at[far],
                    (g, flip(m, far)),
                )
            self.spread(0)

        def wait(self, mask):
            sends, recvs = self.sems
            arrived(self.item(mask), sends.at[mask], recvs.at[mask])

        def forward(self, far):
            self.wait(far)
            self.spread(far)

        def cross(self, far):
            mask = far + 3
            for near, sems, start in ((1, self.sems, 0), (2, self.sems2, half)):
                self.wait(far + near)
                if far not in early:
                    continue
                send(
                    self.buf.at[rows_of(far + near, start, half)],
                    self.buf.at[rows_of(mask, start, half)],
                    sems[0].at[mask],
                    sems[1].at[mask],
                    (g, flip(m, 3 - near)),
                )

        def close(self):
            for far in [0] + fars:
                mask = far + 3
                if far not in early:
                    self.wait(mask)
                    continue
                for sems, start in ((self.sems, 0), (self.sems2, half)):
                    item = self.buf.at[rows_of(mask, start, half)]
                    arrived(item, sems[0].at[mask], sems[1].at[mask])

    def exchange(src_of, buf, send_sems, recv_sems):
        for mask in range(1, blks):
            peer = flip(g, mask)
            send(src_of(peer), buf.at[g], send_sems.at[mask], recv_sems.at[mask], (peer, m))

    def exchanged(buf, send_sems, recv_sems):
        for mask in range(1, blks):
            arrived(buf.at[flip(g, mask)], send_sems.at[mask], recv_sems.at[mask])

    deep = line * block
    tall = min(2, blks) * block

    def gain(buf, near, out):
        span = slice(near * deep, (near + 1) * deep)
        for top in range(0, blks * block, tall):
            term = jnp.dot(
                dense[top : top + tall, span],
                buf[span, :],
                preferred_element_type=jnp.float32,
            ).reshape(tall // block, block, width)
            groups = pl.ds(top // block, tall // block)
            if near == 0:
                out[groups, :block] = term
            else:
                out[groups, :block] += term

    def tally(near):
        for far in [0] + fars:
            mask = near + far
            sums[flip(m, mask)] = jnp.sum(
                pbuf[rows_of(mask), :].astype(jnp.float32).reshape(block // 8, 8, width),
                axis=0,
            )

    xs = Gather(xbuf, x_send, x_recv, x_send2, x_recv2)
    xs.open()
    for fetch in fetches[1:]:
        fetch.wait()
    lax.fori_loop(0, line, lay, 0)
    for far in fars:
        xs.forward(far)
        if far - PLANE in early:
            xs.cross(far - PLANE)
    lax.fori_loop(line, 2 * line, lay, 0)
    gain(xbuf, 0, part)
    for far in fars:
        if far not in early:
            xs.cross(far)
    lax.fori_loop(2 * line, 4 * line, lay, 0)
    gain(xbuf, 1, part)
    gain(xbuf, 2, part)
    xs.close()
    gain(xbuf, 3, part)
    exchange(lambda peer: part.at[peer], ybuf, y_send, y_recv)
    y = part[g]
    exchanged(ybuf, y_send, y_recv)
    for mask in range(1, blks):
        y = y + ybuf[flip(g, mask)]
    high = y.astype(jnp.bfloat16)
    low = (y - high.astype(jnp.float32)).astype(jnp.bfloat16)
    weight = w_own[...]
    pre = (
        jnp.dot(high, weight, preferred_element_type=jnp.float32)
        + jnp.dot(low, weight, preferred_element_type=jnp.float32)
        + b_own[...]
    )
    square = pre * pre
    bent = jnp.tanh(0.7978845608 * (pre + 0.044715 * (square * pre)))
    gate = 0.5 * (1.0 + bent)
    slope = gate + (0.5 * pre) * ((1.0 - bent) * (1.0 + bent)) * (
        0.7978845608 * (1.0 + 0.134145 * square)
    )
    pulled = (ct_own[...].astype(jnp.float32) * slope).astype(jnp.bfloat16)

    pbuf[rows_of(0), :] = pulled
    forward_sends = pending[:]
    del pending[:]
    ps = Gather(pbuf, p_send, p_recv, p_send2, p_recv2)
    ps.open()
    turned = (((0,), (0,)), ((), ()))
    grad = lax.dot_general(high, pulled, turned, preferred_element_type=jnp.float32)
    grad = grad + lax.dot_general(low, pulled, turned, preferred_element_type=jnp.float32)
    chunk = gpart.shape[2]
    count = width // chunk
    chunks = blks * team
    whole = grad.reshape(count, chunk, width)
    if count < chunks:
        empty = jnp.zeros((chunks - count, chunk, width), jnp.float32)
        whole = jnp.concatenate([whole, empty], axis=0)
    gpart[...] = whole.reshape(blks, team, chunk, width)
    exchange(lambda peer: gpart.at[peer], gl1, l1_send, l1_recv)
    ps.forward(fars[0])

    exchanged(gl1, l1_send, l1_recv)
    total = gpart[g]
    for mask in range(1, blks):
        total = total + gl1[flip(g, mask)]
    gtot[...] = total
    for mask in range(1, team):
        peer = flip(m, mask)
        send(gtot.at[peer], grs.at[m], rs_send.at[mask], rs_recv.at[mask], (g, peer))
    grs[m] = gtot[m]
    hidden_ref[...] = (pre * gate).astype(jnp.bfloat16)

    ps.cross(0)
    for far in fars[1:]:
        ps.forward(far)
        if far - PLANE in early:
            ps.cross(far - PLANE)
    for mask in range(1, team):
        arrived(grs.at[flip(m, mask)], rs_send.at[mask], rs_recv.at[mask])
    gag[g, m] = jnp.sum(grs[...], axis=0)
    for mask in range(1, team):
        item = gag.at[g, m]
        send(item, item, ag_send.at[mask], ag_recv.at[mask], (g, flip(m, mask)))
    for copy in forward_sends:
        copy.wait_send()
    gain(pbuf, 0, back)
    tally(0)
    for far in fars:
        if far not in early:
            ps.cross(far)
    gain(pbuf, 1, back)
    gain(pbuf, 2, back)
    tally(1)
    tally(2)
    ps.close()
    gain(pbuf, 3, back)
    tally(3)
    for r in range(blks):
        back[r, block:] = jnp.sum(sums[...], axis=0)
    earlier = pending[:]
    del pending[:]
    exchange(lambda peer: back.at[peer], sbuf, s_send, s_recv)
    for mask in range(1, team):
        arrived(gag.at[g, flip(m, mask)], ag_send.at[mask], ag_recv.at[mask])
    exchange(lambda peer: gag.at[g], gag, l4_send, l4_recv)
    for copy in earlier:
        copy.wait_send()
    spread = back[g]
    exchanged(sbuf, s_send, s_recv)
    for mask in range(1, blks):
        spread = spread + sbuf[flip(g, mask)]
    gi_ref[...] = lax.dot_general(
        spread[:block].astype(jnp.bfloat16),
        weight,
        (((1,), (1,)), ((), ())),
        preferred_element_type=jnp.float32,
    ).astype(jnp.bfloat16)
    gb_ref[...] = jnp.sum(spread[block:], axis=0, keepdims=True)
    exchanged(gag, l4_send, l4_recv)
    gw_ref[...] = gag[...].reshape(chunks * chunk, width)[:width]
    for copy in pending:
        copy.wait_send()


def hand_out(*refs):
    count = len(refs) // 3
    takes, gives, slots, (into, out) = (
        refs[:count],
        refs[count : 2 * count],
        refs[2 * count : 3 * count],
        refs[3 * count :],
    )
    first = [pltpu.make_async_copy(takes[i], slots[i], into.at[i]) for i in range(count)]
    second = [pltpu.make_async_copy(slots[i], gives[i], out.at[i]) for i in range(count)]
    for copy in first:
        copy.start()
    for copy, onward in zip(first, second):
        copy.wait()
        onward.start()
    for copy in second:
        copy.wait()


def local(blks, team, features, weight, bias, cotangent, adj_cols, adj_vals):
    block, width = features.shape
    chunk = 8 * pl.cdiv(width, 8 * blks * team)
    f32, bf16 = jnp.float32, jnp.bfloat16
    dma = pltpu.SemaphoreType.DMA
    vmem = pl.BlockSpec(memory_space=pltpu.VMEM)
    anywhere = pl.BlockSpec(memory_space=pl.ANY)
    panels = blks * block
    outs = (
        jax.ShapeDtypeStruct((block, width), bf16),
        jax.ShapeDtypeStruct((block, width), bf16),
        jax.ShapeDtypeStruct((width, width), f32),
        jax.ShapeDtypeStruct((1, width), f32),
    )
    buffers = [
        ((width, width), bf16),
        ((1, width), f32),
        ((block, width), bf16),
        (adj_vals.shape, bf16),
        ((panels, team * block), bf16),
        ((team * block, width), bf16),
        ((team * block, width), bf16),
        ((blks, block, width), f32),
        ((blks, block + 8, width), f32),
        ((blks, block, width), f32),
        ((blks, block + 8, width), f32),
        ((blks, team, chunk, width), f32),
        ((blks, team, chunk, width), f32),
        ((team, chunk, width), f32),
        ((team, chunk, width), f32),
        ((blks, team, chunk, width), f32),
        ((team, 8, width), f32),
    ]
    results = pl.pallas_call(
        functools.partial(kernel, blks, team),
        out_shape=outs,
        in_specs=[anywhere] * 6,
        out_specs=(vmem,) * 4,
        scratch_shapes=[pltpu.VMEM(shape, kind) for shape, kind in buffers[:3]]
        + [pltpu.SMEM(adj_cols.shape, jnp.int32)]
        + [pltpu.VMEM(shape, kind) for shape, kind in buffers[3:]]
        + [dma((6,))]
        + [dma((team,))] * 8
        + [dma((blks,))] * 6
        + [dma((team,))] * 4
        + [dma((blks,))] * 2,
        compiler_params=pltpu.CompilerParams(
            collective_id=0, has_side_effects=True, vmem_limit_bytes=56 * 2**20
        ),
    )(features, weight, bias.reshape(1, width), cotangent, adj_cols, adj_vals)
    hidden, grad_input, grad_weight, grad_bias = pl.pallas_call(
        hand_out,
        out_shape=outs,
        in_specs=[anywhere] * 4,
        out_specs=(anywhere,) * 4,
        scratch_shapes=[pltpu.VMEM(out.shape, out.dtype) for out in outs]
        + [dma((4,)), dma((4,))],
        compiler_params=pltpu.CompilerParams(vmem_limit_bytes=56 * 2**20),
    )(*results)
    return hidden, grad_input, grad_weight, grad_bias.reshape(width)


def solution(mesh):
    return jax.shard_map(
        functools.partial(local, mesh.shape["blk"], mesh.shape["team"]),
        mesh=mesh,
        in_specs=(
            P(("blk", "team"), None),
            P(),
            P(),
            P(("blk", "team"), None),
            P("team", None, "blk", None),
            P("team", None, "blk", None, None, None),
        ),
        out_specs=(P(("blk", "team"), None), P(("blk", "team"), None), P(), P()),
        check_vma=False,
    )
```
